256 devices in a mesh: tm: 8 (over y, core), space: 32 (over x, z).
Axes of the slice: x: 4, y: 4, z: 8, core: 2. Of those that a mesh axis runs over, the one named last changes fastest.
Arguments:
- snapshots: bfloat16 [8192, 12, 32, 256], P('tm', None, 'space'), may hold values from -6 to 6
- sketch: bfloat16 [8192, 256], P('tm'), may hold values from -0.0625 to 0.0625
- volume: float32 [32, 256], P('space'), may hold values from 0.3 to 27, as said below
- grad_weight: float32 [12], replicated, may hold values from 0.5 to 2
- dilation: int32 [12], replicated, may hold values from 1 to 4
Outputs:
- basis: float32 [256, 12, 32, 256], P('tm', None, 'space')
- upper: float32 [256, 256], replicated
The draws below stay inside these ranges and needn't reach their ends.
Inputs may be any that keep to these rules, and one draw needn't show every extreme that they name: `volume`: positive cell volumes.
All inputs are finite; a program needn't handle non-finite values.
Results may differ from the reference program's by a relative error of at most 0.0003.
Values sent between devices are 32-bit elements; how exact they have to be, the bound alone decides.
No kernel may reach another device: no remote copies, remote signals or barrier semaphores. Data moves between devices by JAX's collectives and lax.ppermute only.
A program may use at most 128 MiB of HBM per device.

```python
import math
import jax
import jax.numpy as jnp
from jax import lax

FIELDS = 12
RANK = 256
WX = 16
WY = 16
SNAP_DEV = 1024
PLANE = 256
NZ = 32
SNAPS = 8192
ROWS = 98304
N_TM = 8


def draw_volume(key, part):
    key = jax.random.fold_in(key, 7)
    level = jnp.arange(NZ, dtype=jnp.float32)[:, None] / max(NZ - 1, 1)
    overall = jnp.exp(jax.random.uniform(jax.random.fold_in(key, 1), (), jnp.float32, jnp.log(0.6), jnp.log(1.6)))
    cell_key = jax.random.fold_in(key, 2)
    base = jnp.exp(jnp.log(3.0) * level)
    noise = jnp.exp(jax.random.uniform(cell_key, (NZ, PLANE), jnp.float32, jnp.log(0.5), jnp.log(2.0)))
    return (overall * base * noise).astype(jnp.float32)


def place_ends(drawn, rng, smallest, largest):
    extent = drawn.shape
    place = [jax.random.randint(jax.random.fold_in(rng, axis), (), 0, extent[axis]) for axis in range(len(extent))]
    drawn = drawn.at[tuple(place)].set(smallest)
    longest = extent.index(max(extent))
    place[longest] = (place[longest] + 1) % extent[longest]
    return drawn.at[tuple(place)].set(largest)


def block_levels(key, shape, cuts, least, largest):
    factor_of = 1.0
    for dim, parts in cuts:
        heights = jax.random.uniform(jax.random.fold_in(jax.random.fold_in(key, 6), dim), (parts,), jnp.float32, least / len(cuts), largest / len(cuts))
        factor_of = factor_of * jnp.repeat(jnp.exp(heights), shape[dim] // parts).reshape((-1,) + (1,) * (len(shape) - 1 - dim))
    return factor_of


def scatter_about(stream_key, extent, width, most, cuts=(), held_as=jnp.bfloat16):
    array = width * jax.random.normal(stream_key, extent, jnp.float32)
    if cuts:
        array = array * block_levels(stream_key, extent, cuts, -0.22, 0.18)
    return jnp.clip(array, -most, most).astype(held_as)


def setup_inputs(seed: int = 0) -> dict:
    arg_keys = jax.random.split(jax.random.key(seed), 6)
    snapshots = scatter_about(arg_keys[0], (SNAPS, FIELDS, NZ, PLANE), 1.0, 6.0, ((0, 8), (2, 32)))
    sketch = scatter_about(arg_keys[1], (SNAPS, RANK), SNAPS ** -0.5, 0.0625, ((0, 8),))
    volume = draw_volume(jax.random.fold_in(arg_keys[5], 71), 0)
    grad_weight = jnp.clip(jnp.exp(jax.random.uniform(arg_keys[3], (FIELDS,), jnp.float32, math.log(0.5), math.log(2.0))), 0.5, 2.0)
    dilation = place_ends(jax.random.randint(arg_keys[4], (FIELDS,), 1, 5), jax.random.fold_in(arg_keys[4], 1), 1, 4).astype(jnp.int32)
    return dict(snapshots=snapshots, sketch=sketch, volume=volume, grad_weight=grad_weight, dilation=dilation)


def line_ops(length, dilation):
    row_index = jnp.arange(length, dtype=jnp.int32)[:, None]
    col_index = jnp.arange(length, dtype=jnp.int32)[None, :]
    blur_line = jnp.where(row_index == col_index, jnp.float32(0.5), jnp.float32(0.0))
    blur_line = blur_line + jnp.where(jnp.abs(row_index - col_index) == 1, jnp.float32(0.25), jnp.float32(0.0))
    shift_by = dilation[:, None, None]
    diff_line = jnp.where(col_index[None] == row_index[None] + shift_by, jnp.float32(0.5), jnp.float32(0.0))
    diff_line = diff_line - jnp.where(col_index[None] == row_index[None] - shift_by, jnp.float32(0.5), jnp.float32(0.0))
    return (blur_line, diff_line)

def filter_matrix(dilation, grad_weight):
    blur_x, diff_x = line_ops(WX, dilation)
    blur_y, diff_y = line_ops(WY, dilation)
    blur = jnp.kron(blur_y, blur_x)
    eye_x = jnp.eye(WX, dtype=jnp.float32)
    eye_y = jnp.eye(WY, dtype=jnp.float32)

    def one_field(diff_xf, diff_yf):
        return jnp.kron(eye_y, diff_xf) + jnp.kron(diff_yf, eye_x)
    gradient = jax.vmap(one_field)(diff_x, diff_y)
    mixed = jnp.einsum('fqr,rp->fqp', gradient, blur, precision=lax.Precision.HIGHEST)
    return blur[None] + grad_weight[:, None, None] * mixed

def reference(snapshots, sketch, volume, grad_weight, dilation):
    matrix = filter_matrix(dilation, grad_weight)
    sketch_f = sketch.astype(jnp.float32).reshape(N_TM, SNAP_DEV, RANK)

    def one_plane(level):
        picked = lax.dynamic_index_in_dim(snapshots, level.astype(jnp.int32), axis=2, keepdims=False)
        picked = picked.astype(jnp.float32).reshape(N_TM, SNAP_DEV, FIELDS, PLANE)
        group_parts = jnp.einsum('gsfp,gsk->gpfk', picked, sketch_f, precision=lax.Precision.HIGHEST)
        raw = jnp.sum(group_parts, axis=0)
        return jnp.einsum('fqp,pfk->qfk', matrix, raw, precision=lax.Precision.HIGHEST)
    images = lax.map(one_plane, jnp.arange(NZ, dtype=jnp.int32))
    padded = jnp.pad(images, ((1, 1), (0, 0), (0, 0), (0, 0)))
    planes = 0.25 * padded[0:NZ] + 0.5 * padded[1:NZ + 1] + 0.25 * padded[2:NZ + 2]
    panel = jnp.transpose(planes, (1, 2, 0, 3))
    panel_rows = panel.reshape(-1, RANK)
    weighted = (panel * jnp.transpose(volume)[:, None, :, None]).reshape(-1, RANK)
    gram_matrix = jnp.dot(weighted.T.astype(jnp.float32), panel_rows.astype(jnp.float32), precision=lax.Precision.HIGHEST, preferred_element_type=jnp.float32) / ROWS
    lower_factor = jnp.linalg.cholesky(gram_matrix)
    basis_rows = lax.linalg.triangular_solve(lower_factor, panel_rows, left_side=False, lower=True, transpose_a=True)
    return (basis_rows.reshape(panel.shape), jnp.transpose(lower_factor))
```

```python
import functools

import jax
import jax.numpy as jnp
from jax import lax
from jax.experimental import pallas as pl
from jax.experimental.pallas import tpu as pltpu
from jax.sharding import PartitionSpec as P

WX = 16
WY = 16
PLANE = WX * WY
RANK = 256
FIELDS = 12
SHARE = 32
NZ = 32
ROWS = 98304
HALF = 128
EXACT = lax.Precision.HIGHEST


def hat(offset):
    return jnp.maximum(0.5 - 0.25 * jnp.abs(offset), 0.0)


def hat_slope(source, target, shift):
    ahead = jnp.where(target + shift < 16.0, hat(source - target - shift), 0.0)
    behind = jnp.where(target - shift >= 0.0, hat(source - target + shift), 0.0)
    return 0.5 * (ahead - behind)


def filter_rows(out_ref, blocks, shift, weight):
    lane = lax.broadcasted_iota(jnp.int32, (WX, PLANE), 1)
    px = (lane % WX).astype(jnp.float32)
    py = (lane[:8] // WX).astype(jnp.float32)
    qx = lax.broadcasted_iota(jnp.int32, (WX, PLANE), 0).astype(jnp.float32)
    along_x = hat(px - qx)
    mixed_x = along_x + weight * hat_slope(px, qx, shift)
    for r, block in enumerate(blocks):
        for h in range(2):
            qy = jnp.full((8, PLANE), (2 * block + h).astype(jnp.float32))
            along_y = hat(py - qy)
            slope_y = weight * hat_slope(py, qy, shift)
            for g in range(2):
                rows = slice(8 * g, 8 * g + 8)
                out_ref[pl.ds(32 * r + 16 * h + 8 * g, 8), :] = (
                    along_y * mixed_x[rows] + slope_y * along_x[rows]
                )


def split(x):
    high = x.astype(jnp.bfloat16)
    return high, (x - high.astype(jnp.float32)).astype(jnp.bfloat16)


def sketch_kernel(
    first, order, dilation, weight, snap_ref, sketch_ref, send_ref, keep_ref, turned, matrix
):
    step = pl.program_id(0)
    me = lax.axis_index("tm")
    y, core = me // 2, me % 2

    @pl.when(step == 0)
    def _():
        turned[...] = sketch_ref[...].T

    blocks = [2 * (y ^ m) + (1 - core) for m in order] + [2 * (y ^ m) + core for m in order]
    filter_rows(
        matrix, blocks, dilation[first + step].astype(jnp.float32), weight[first + step]
    )
    raw = jnp.dot(turned[...], snap_ref[0], preferred_element_type=jnp.float32)
    raw_high, raw_low = split(raw)
    mat_high, mat_low = split(matrix[...])
    dot = functools.partial(
        lax.dot_general,
        dimension_numbers=(((1,), (1,)), ((), ())),
        preferred_element_type=jnp.float32,
    )
    image = dot(mat_high, raw_high) + (dot(mat_high, raw_low) + dot(mat_low, raw_high))
    send_ref[:, 0] = image[:HALF].reshape(4, SHARE, RANK)
    keep_ref[:, 0] = image[HALF:].reshape(4, SHARE, RANK)


def sketch_call(snaps, sketch, dilation, weight, first, count, order):
    out = jax.ShapeDtypeStruct((4, count, SHARE, RANK), jnp.float32)
    smem = pl.BlockSpec(memory_space=pltpu.SMEM)
    return pl.pallas_call(
        functools.partial(sketch_kernel, first, order),
        grid=(count,),
        in_specs=[
            smem,
            smem,
            pl.BlockSpec((1, 1024, PLANE), lambda i: (first + i, 0, 0)),
            pl.BlockSpec((1024, RANK), lambda i: (0, 0)),
        ],
        out_specs=[pl.BlockSpec((4, 1, SHARE, RANK), lambda i: (0, i, 0, 0))] * 2,
        out_shape=[out, out],
        scratch_shapes=[
            pltpu.VMEM((RANK, 1024), jnp.bfloat16),
            pltpu.VMEM((PLANE, PLANE), jnp.float32),
        ],
        compiler_params=pltpu.CompilerParams(vmem_limit_bytes=16 * 2**20),
        cost_estimate=pl.CostEstimate(
            flops=count * 2 * 256 * 256 * 1792, bytes_accessed=count * 2**20, transcendentals=0
        ),
    )(dilation, weight, snaps, sketch)


def panel_kernel(counts, volume_ref, *refs):
    parts, (panel_ref, gram_ref) = refs[:-2], refs[-2:]
    me, plane = lax.axis_index("tm"), lax.axis_index("space")
    row = lax.broadcasted_iota(jnp.int32, (SHARE, PLANE), 0)
    lane = lax.broadcasted_iota(jnp.int32, (SHARE, PLANE), 1)
    volume = jnp.broadcast_to(volume_ref[...], (SHARE, PLANE))
    mine = jnp.sum(jnp.where(lane == row + me * SHARE, volume, 0.0), axis=1, keepdims=True)
    root = jnp.broadcast_to(jnp.sqrt(mine), (SHARE, RANK))
    scaled = []
    at = 0
    for n, count in enumerate(counts):
        here, below, above = parts[3 * n : 3 * n + 3]
        for f in range(count):
            panel = 0.5 * here[f]
            panel = panel + jnp.where(plane > 0, 0.25 * below[f], 0.0)
            panel = panel + jnp.where(plane < NZ - 1, 0.25 * above[f], 0.0)
            panel_ref[at] = panel
            scaled.append(panel * root)
            at += 1
    rows = jnp.concatenate(scaled, axis=0)
    gram = lax.dot_general(
        rows,
        rows,
        (((0,), (0,)), ((), ())),
        precision=EXACT,
        preferred_element_type=jnp.float32,
    )
    gram = gram * (1.0 / ROWS)
    gram_ref[:HALF] = gram[HALF:, :HALF]
    row = lax.broadcasted_iota(jnp.int32, (HALF, HALF), 0)
    lane = lax.broadcasted_iota(jnp.int32, (HALF, HALF), 1)
    last = gram[HALF:, HALF:]
    gram_ref[HALF : 2 * HALF] = jnp.where(row >= lane, gram[:HALF, :HALF], last)
    diag = jnp.sum(jnp.where(row == lane, last, 0.0), axis=0, keepdims=True)
    gram_ref[2 * HALF :] = jnp.broadcast_to(diag, (16, HALF))


def panel_call(volume, counts, parts):
    vmem = pl.BlockSpec(memory_space=pltpu.VMEM)
    return pl.pallas_call(
        functools.partial(panel_kernel, counts),
        in_specs=[vmem] * (1 + len(parts)),
        out_specs=[vmem, vmem],
        out_shape=[
            jax.ShapeDtypeStruct((FIELDS, SHARE, RANK), jnp.float32),
            jax.ShapeDtypeStruct((272, HALF), jnp.float32),
        ],
        compiler_params=pltpu.CompilerParams(vmem_limit_bytes=16 * 2**20),
    )(volume, *parts)


def factor(rows):
    shape = (8, HALF)
    sub = lax.broadcasted_iota(jnp.int32, shape, 0)
    lane = lax.broadcasted_iota(jnp.int32, shape, 1)
    rows = list(rows)
    count = len(rows)
    inverse = [jnp.where(lane == sub + 8 * t, 1.0, 0.0) for t in range(count)]
    uppers, lowers = [], []

    def column(x, j):
        return jnp.broadcast_to(x[:, j : j + 1], shape)

    def row_of(x, i):
        return jnp.broadcast_to(x[i : i + 1, :], shape)

    def total(terms):
        terms = list(terms)
        while len(terms) > 1:
            terms = [a + b for a, b in zip(terms[::2], terms[1::2])] + (
                terms[-1:] if len(terms) % 2 else []
            )
        return terms[0]

    def stack(parts):
        out = parts[-1]
        for i in range(len(parts) - 2, -1, -1):
            out = jnp.where(sub == i, parts[i], out)
        return out

    for s in range(count):
        here, there = rows[s], inverse[s]
        cols = [column(here, 8 * s + m) for m in range(8)]
        d = {(i, m): row_of(cols[m], i) for m in range(8) for i in range(m, 8)}
        low, root = {}, []
        for j in range(8):
            root.append(lax.rsqrt(d[j, j]))
            for i in range(j + 1, 8):
                low[i, j] = d[i, j] * root[j]
            for k in range(j + 1, 8):
                for i in range(k, 8):
                    d[i, k] = d[i, k] - low[i, j] * low[k, j]
        inv = {}
        for j in range(8):
            inv[j, j] = root[j]
            for i in range(j + 1, 8):
                inv[i, j] = -root[i] * total(low[i, k] * inv[k, j] for k in range(j, i))
        here_rows = [row_of(here, m) for m in range(8)]
        there_rows = [row_of(there, m) for m in range(8)]
        zero = jnp.zeros(shape, jnp.float32)
        lower_cols = [stack([inv[i, m] if i >= m else zero for i in range(8)]) for m in range(8)]
        upper = total(lower_cols[m] * here_rows[m] for m in range(8))
        uppers.append(jnp.where(lane >= sub + 8 * s, upper, 0.0))
        lowers.append(total(lower_cols[m] * there_rows[m] for m in range(8)))
        if s + 1 == count:
            break
        full = {}
        for i in range(8):
            for j in range(i + 1):
                full[i, j] = full[j, i] = total(inv[k, i] * inv[k, j] for k in range(i, 8))
        full_cols = [stack([full[i, m] for i in range(8)]) for m in range(8)]
        solved = total(full_cols[m] * here_rows[m] for m in range(8))
        solved_inv = total(full_cols[m] * there_rows[m] for m in range(8))
        solved_rows = [row_of(solved, m) for m in range(8)]
        inv_rows = [row_of(solved_inv, m) for m in range(8)]
        for t in range(s + 1, count):
            weights = [column(rows[t], 8 * s + m) for m in range(8)]
            rows[t] = rows[t] - total(weights[m] * solved_rows[m] for m in range(8))
            inverse[t] = inverse[t] - total(weights[m] * inv_rows[m] for m in range(8))
    return uppers, lowers


def basis_kernel(gram_ref, panel_ref, basis_ref, upper_ref, lower):
    row = lax.broadcasted_iota(jnp.int32, (HALF, HALF), 0)
    lane = lax.broadcasted_iota(jnp.int32, (HALF, HALF), 1)
    cross = gram_ref[:HALF]
    mixed = gram_ref[HALF : 2 * HALF]
    turned = mixed.T
    first = jnp.where(row >= lane, mixed, turned)
    diag = jnp.broadcast_to(gram_ref[2 * HALF : 2 * HALF + 1, :], (HALF, HALF))
    last = jnp.where(row < lane, mixed, jnp.where(row > lane, turned, diag))

    def dot(a, b, da, db):
        return lax.dot_general(
            a,
            b,
            (((da,), (db,)), ((), ())),
            precision=EXACT,
            preferred_element_type=jnp.float32,
        )

    groups = range(HALF // 8)
    uppers, lowers = factor([first[8 * t : 8 * t + 8] for t in groups])
    low_a = jnp.concatenate(lowers, axis=0)
    upper_ref[:HALF, :HALF] = jnp.concatenate(uppers, axis=0)
    side = dot(low_a, cross, 1, 1)
    upper_ref[:HALF, HALF:] = side
    upper_ref[HALF:, :HALF] = jnp.zeros((HALF, HALF), jnp.float32)
    last = last - dot(side, side, 0, 0)
    uppers, lowers = factor([last[8 * t : 8 * t + 8] for t in groups])
    low_b = jnp.concatenate(lowers, axis=0)
    upper_ref[HALF:, HALF:] = jnp.concatenate(uppers, axis=0)
    lower[:HALF, :HALF] = low_a
    lower[:HALF, HALF:] = jnp.zeros((HALF, HALF), jnp.float32)
    lower[HALF:, :HALF] = -dot(low_b, dot(side, low_a, 0, 0), 1, 0)
    lower[HALF:, HALF:] = low_b
    for f in range(FIELDS):
        basis_ref[:, f, 0, :] = dot(panel_ref[f], lower[...], 1, 1)


def basis_call(gram, panel):
    vmem = pl.BlockSpec(memory_space=pltpu.VMEM)
    return pl.pallas_call(
        basis_kernel,
        in_specs=[vmem, vmem],
        out_specs=[vmem, vmem],
        out_shape=[
            jax.ShapeDtypeStruct((SHARE, FIELDS, 1, RANK), jnp.float32),
            jax.ShapeDtypeStruct((RANK, RANK), jnp.float32),
        ],
        scratch_shapes=[pltpu.VMEM((RANK, RANK), jnp.float32)],
        compiler_params=pltpu.CompilerParams(vmem_limit_bytes=32 * 2**20),
    )(gram, panel)


def swap(x, axis, mask):
    return lax.ppermute(x, axis, [(i, i ^ mask) for i in range(lax.axis_size(axis))])


def ring(x, axis, step):
    n = lax.axis_size(axis)
    return lax.ppermute(x, axis, [(i, (i + step) % n) for i in range(n)])


def sum_over_tm(send, keep, near, far):
    got = swap(send, "tm", 1)
    mine = keep + got
    got = swap(mine[2:], "tm", 2 * near)
    mine = mine[:2] + got
    got = swap(mine[1], "tm", 2 * far)
    return mine[0] + got


def sum_over_all(gram):
    core = lax.axis_index("tm") % 2
    n = gram.shape[0] // 2
    mine = lax.dynamic_slice_in_dim(gram, core * n, n, 0)
    other = lax.dynamic_slice_in_dim(gram, (1 - core) * n, n, 0)
    mine = mine + swap(other, "tm", 1)
    for mask in (2, 6):
        mine = mine + swap(mine, "tm", mask)
    for mask in (8, 24, 1, 2, 7):
        mine = mine + swap(mine, "space", mask)
    other = swap(mine, "tm", 1)
    return jnp.where(
        core == 0, jnp.concatenate([mine, other], 0), jnp.concatenate([other, mine], 0)
    )


def shards(snapshots, sketch, volume, grad_weight, dilation):
    snaps = jnp.transpose(snapshots[:, :, 0, :], (1, 0, 2))
    counts = (6, 6)
    parts = []
    first = 0
    for count, (near, far) in zip(counts, ((1, 3), (3, 1))):
        order = (0, far, near, near ^ far)
        send, keep = sketch_call(snaps, sketch, dilation, grad_weight, first, count, order)
        image = sum_over_tm(send, keep, near, far)
        parts += [image, ring(image, "space", 1), ring(image, "space", -1)]
        first += count
    panel, gram = panel_call(volume, counts, parts)
    gram = sum_over_all(gram)
    basis, upper = basis_call(gram, panel)
    return basis, upper


def solution(mesh):
    return jax.shard_map(
        shards,
        mesh=mesh,
        in_specs=(P("tm", None, "space", None), P("tm", None), P("space", None), P(), P()),
        out_specs=(P("tm", None, "space", None), P()),
        check_vma=False,
    )
```

```python
import functools

import jax
import jax.numpy as jnp
from jax import lax
from jax.experimental import pallas as pl
from jax.experimental.pallas import tpu as pltpu
from jax.sharding import PartitionSpec as P

WX = 16
WY = 16
PLANE = WX * WY
RANK = 256
FIELDS = 12
SHARE = 32
SNAP_DEV = 1024
NZ = 32
ROWS = 98304
HALF = 128
GROUP = 4
DILATIONS = 4
EXACT = lax.Precision.HIGHEST


def hat(offset):
    return jnp.maximum(0.5 - 0.25 * jnp.abs(offset), 0.0)


def hat_slope(source, target, shift):
    ahead = jnp.where(target + shift < 16.0, hat(source - target - shift), 0.0)
    behind = jnp.where(target - shift >= 0.0, hat(source - target + shift), 0.0)
    return 0.5 * (ahead - behind)


def filter_tables(table, blocks):
    lane = lax.broadcasted_iota(jnp.int32, (WX, PLANE), 1)
    px = (lane & 15).astype(jnp.float32)
    py = (lane >> 4).astype(jnp.float32)
    qx = lax.broadcasted_iota(jnp.int32, (WX, PLANE), 0).astype(jnp.float32)
    along_x = hat(px - qx)
    slopes = [hat_slope(px, qx, float(d + 1)) for d in range(DILATIONS)]
    for r, block in enumerate(blocks):
        for h in range(2):
            qy = jnp.full((WX, PLANE), (2 * block + h).astype(jnp.float32))
            rows = pl.ds(32 * r + 16 * h, 16)
            along_y = hat(py - qy)
            table[0, rows, :] = (along_y * along_x).astype(jnp.bfloat16)
            for d in range(DILATIONS):
                mixed = along_y * slopes[d] + hat_slope(py, qy, float(d + 1)) * along_x
                table[d + 1, rows, :] = mixed.astype(jnp.bfloat16)


def split(x):
    high = x.astype(jnp.bfloat16)
    return high, (x - high.astype(jnp.float32)).astype(jnp.bfloat16)


def sketch_kernel(orders, snap_hbm, sketch_hbm, shift_hbm, weight_hbm, *refs):
    outs = refs[: 2 * len(orders)]
    snap, sketch, turned, table, shift, weight, snap_sem, sem = refs[2 * len(orders) :]
    first = [
        pltpu.make_async_copy(sketch_hbm, sketch, sem.at[0]),
        pltpu.make_async_copy(shift_hbm, shift, sem.at[1]),
        pltpu.make_async_copy(weight_hbm, weight, sem.at[2]),
    ]
    copies = [
        pltpu.make_async_copy(snap_hbm.at[f], snap.at[f], snap_sem.at[f]) for f in range(FIELDS)
    ]
    for copy in first + copies:
        copy.start()
    me = lax.axis_index("tm")
    y, core = me // 2, me % 2
    order = orders[0]
    filter_tables(
        table, [2 * (y ^ m) + (1 - core) for m in order] + [2 * (y ^ m) + core for m in order]
    )
    for copy in first:
        copy.wait()
    turned[...] = sketch[...].T
    each = FIELDS // len(orders)
    dot = functools.partial(
        lax.dot_general,
        dimension_numbers=(((1,), (1,)), ((), ())),
        preferred_element_type=jnp.float32,
    )

    def filtered(f, raw):
        high, low = split(raw)
        blur, slope = table[0], table[shift[f]]
        image = (dot(blur, high) + dot(blur, low)) + weight[f] * (
            dot(slope, high) + dot(slope, low)
        )
        n, i = divmod(f, each)
        for r, mask in enumerate(orders[n]):
            at = SHARE * order.index(mask)
            outs[2 * n][r, i] = image[at : at + SHARE]
            outs[2 * n + 1][r, i] = image[HALF + at : HALF + at + SHARE]

    held = None
    for g in range(0, FIELDS + GROUP, GROUP):
        if g < FIELDS:
            for f in range(g, g + GROUP):
                copies[f].wait()
            raws = [
                jnp.dot(turned[...], snap[f], preferred_element_type=jnp.float32)
                for f in range(g, g + GROUP)
            ]
        if held is not None:
            for k in range(GROUP):
                filtered(g - GROUP + k, held[k])
        held = raws


def sketch_call(snaps, sketch, dilation, weight, orders):
    out = jax.ShapeDtypeStruct((4, FIELDS // len(orders), SHARE, RANK), jnp.float32)
    hbm = pl.BlockSpec(memory_space=pltpu.HBM)
    vmem = pl.BlockSpec(memory_space=pltpu.VMEM)
    return pl.pallas_call(
        functools.partial(sketch_kernel, orders),
        in_specs=[hbm] * 4,
        out_specs=[vmem] * (2 * len(orders)),
        out_shape=[out] * (2 * len(orders)),
        scratch_shapes=[
            pltpu.VMEM((FIELDS, SNAP_DEV, PLANE), jnp.bfloat16),
            pltpu.VMEM((SNAP_DEV, RANK), jnp.bfloat16),
            pltpu.VMEM((RANK, SNAP_DEV), jnp.bfloat16),
            pltpu.VMEM((DILATIONS + 1, PLANE, PLANE), jnp.bfloat16),
            pltpu.SMEM((FIELDS,), jnp.int32),
            pltpu.SMEM((FIELDS,), jnp.float32),
            pltpu.SemaphoreType.DMA((FIELDS,)),
            pltpu.SemaphoreType.DMA((3,)),
        ],
        compiler_params=pltpu.CompilerParams(vmem_limit_bytes=52 * 2**20),
    )(snaps, sketch, dilation, weight)


def panel_kernel(counts, volume_ref, *refs):
    parts, (panel_ref, gram_ref) = refs[:-2], refs[-2:]
    me, plane = lax.axis_index("tm"), lax.axis_index("space")
    row = lax.broadcasted_iota(jnp.int32, (SHARE, PLANE), 0)
    lane = lax.broadcasted_iota(jnp.int32, (SHARE, PLANE), 1)
    volume = jnp.broadcast_to(volume_ref[...], (SHARE, PLANE))
    mine = jnp.sum(jnp.where(lane == row + me * SHARE, volume, 0.0), axis=1, keepdims=True)
    root = jnp.broadcast_to(jnp.sqrt(mine), (SHARE, RANK))
    scaled = []
    at = 0
    for n, count in enumerate(counts):
        here, below, above = parts[3 * n : 3 * n + 3]
        for f in range(count):
            panel = 0.5 * here[f]
            panel = panel + jnp.where(plane > 0, 0.25 * below[f], 0.0)
            panel = panel + jnp.where(plane < NZ - 1, 0.25 * above[f], 0.0)
            panel_ref[at] = panel
            scaled.append(panel * root)
            at += 1
    rows = jnp.concatenate(scaled, axis=0)
    gram = lax.dot_general(
        rows,
        rows,
        (((0,), (0,)), ((), ())),
        precision=EXACT,
        preferred_element_type=jnp.float32,
    )
    gram = gram * (1.0 / ROWS)
    gram_ref[:HALF] = gram[HALF:, :HALF]
    row = lax.broadcasted_iota(jnp.int32, (HALF, HALF), 0)
    lane = lax.broadcasted_iota(jnp.int32, (HALF, HALF), 1)
    last = gram[HALF:, HALF:]
    gram_ref[HALF : 2 * HALF] = jnp.where(row >= lane, gram[:HALF, :HALF], last)
    diag = jnp.sum(jnp.where(row == lane, last, 0.0), axis=0, keepdims=True)
    gram_ref[2 * HALF :] = jnp.broadcast_to(diag, (16, HALF))


def panel_call(volume, counts, parts):
    vmem = pl.BlockSpec(memory_space=pltpu.VMEM)
    return pl.pallas_call(
        functools.partial(panel_kernel, counts),
        in_specs=[vmem] * (1 + len(parts)),
        out_specs=[vmem, vmem],
        out_shape=[
            jax.ShapeDtypeStruct((FIELDS, SHARE, RANK), jnp.float32),
            jax.ShapeDtypeStruct((272, HALF), jnp.float32),
        ],
        compiler_params=pltpu.CompilerParams(vmem_limit_bytes=16 * 2**20),
    )(volume, *parts)


def total(terms):
    terms = list(terms)
    while len(terms) > 1:
        terms = [a + b for a, b in zip(terms[::2], terms[1::2])] + (
            terms[-1:] if len(terms) % 2 else []
        )
    return terms[0]


def factor(rows):
    shape = (8, HALF)
    sub = lax.broadcasted_iota(jnp.int32, shape, 0)
    lane = lax.broadcasted_iota(jnp.int32, shape, 1)
    rows = list(rows)
    count = len(rows)
    uppers, lowers = [], []
    at = [sub == j for j in range(8)]

    def column(x, j):
        return jnp.broadcast_to(x[:, j : j + 1], shape)

    def row_of(x, i):
        return jnp.broadcast_to(x[i : i + 1, :], shape)

    for s in range(count):
        here = rows[s]
        there = jnp.where(lane == sub + 8 * s, 1.0, 0.0)
        inside = (lane >= 8 * s) & (lane < 8 * s + 8)
        cols = [column(here, 8 * s + m) for m in range(8)]
        upper = lower = jnp.zeros(shape, jnp.float32)
        for j in range(0, 8, 2):
            p, q = cols[j], cols[j + 1]
            a, b, c = row_of(p, j), row_of(q, j), row_of(q, j + 1)
            det = a * c - b * b
            inv_det = 1.0 / det
            inv_a = 1.0 / a
            root_a, root_c = lax.rsqrt(a), lax.rsqrt(det * inv_a)
            slope = b * inv_a

            def eliminate(x, kept=None):
                x0, x1 = row_of(x, j), row_of(x, j + 1)
                y0 = (c * x0 - b * x1) * inv_det
                y1 = (a * x1 - b * x0) * inv_det
                new = jnp.where(at[j], y0, jnp.where(at[j + 1], y1, x - p * y0 - q * y1))
                if kept is None:
                    return new
                second = (x1 - slope * x0) * root_c
                return new, jnp.where(at[j], x0 * root_a, jnp.where(at[j + 1], second, kept))

            here, upper = eliminate(here, upper)
            there, lower = eliminate(there, lower)
            for m in range(j + 2, 8):
                cols[m] = eliminate(cols[m])
        uppers.append(jnp.where(lane >= sub + 8 * s, upper, 0.0))
        lowers.append(jnp.where(inside, lower, jnp.where(lane < 8 * s, upper, 0.0)))
        if s + 1 == count:
            break
        solved = jnp.where(inside, there, here)
        solved_rows = [row_of(solved, m) for m in range(8)]
        for t in range(s + 1, count):
            weights = [column(rows[t], 8 * s + m) for m in range(8)]
            rows[t] = jnp.where(inside, 0.0, rows[t]) - total(
                weights[m] * solved_rows[m] for m in range(8)
            )
    return uppers, lowers


def basis_kernel(gram_ref, panel_ref, basis_ref, upper_ref):
    row = lax.broadcasted_iota(jnp.int32, (HALF, HALF), 0)
    lane = lax.broadcasted_iota(jnp.int32, (HALF, HALF), 1)
    cross = gram_ref[:HALF]
    mixed = gram_ref[HALF : 2 * HALF]
    turned = mixed.T
    first = jnp.where(row >= lane, mixed, turned)
    diag = jnp.broadcast_to(gram_ref[2 * HALF : 2 * HALF + 1, :], (HALF, HALF))
    last = jnp.where(row < lane, mixed, jnp.where(row > lane, turned, diag))
    cells = FIELDS * SHARE

    def dot(a, b, da, db):
        return lax.dot_general(
            a,
            b,
            (((da,), (db,)), ((), ())),
            precision=EXACT,
            preferred_element_type=jnp.float32,
        )

    def put(x, h):
        for f in range(FIELDS):
            basis_ref[pl.ds(2 * f + h, SHARE, stride=2 * FIELDS), :] = x[
                SHARE * f : SHARE * f + SHARE
            ]

    groups = range(HALF // 8)
    uppers, lowers = factor([first[8 * t : 8 * t + 8] for t in groups])
    low_a = jnp.concatenate(lowers, axis=0)
    upper_ref[:HALF, :HALF] = jnp.concatenate(uppers, axis=0)
    side = dot(low_a, cross, 1, 1)
    last = last - dot(side, side, 0, 0)
    upper_ref[:HALF, HALF:] = side
    upper_ref[HALF:, :HALF] = jnp.zeros((HALF, HALF), jnp.float32)
    basis_a = dot(panel_ref[:, :, :HALF].reshape(cells, HALF), low_a, 1, 1)
    rest = panel_ref[:, :, HALF:].reshape(cells, HALF) - dot(basis_a, side, 1, 0)
    put(basis_a, 0)
    uppers, lowers = factor([last[8 * t : 8 * t + 8] for t in groups])
    low_b = jnp.concatenate(lowers, axis=0)
    upper_ref[HALF:, HALF:] = jnp.concatenate(uppers, axis=0)
    put(dot(rest, low_b, 1, 1), 1)


def basis_call(gram, panel):
    vmem = pl.BlockSpec(memory_space=pltpu.VMEM)
    basis, upper = pl.pallas_call(
        basis_kernel,
        in_specs=[vmem, vmem],
        out_specs=[vmem, vmem],
        out_shape=[
            jax.ShapeDtypeStruct((SHARE * FIELDS * 2, HALF), jnp.float32),
            jax.ShapeDtypeStruct((RANK, RANK), jnp.float32),
        ],
        compiler_params=pltpu.CompilerParams(vmem_limit_bytes=32 * 2**20),
    )(gram, panel)
    return basis.reshape(SHARE, FIELDS, 1, RANK), upper


def swap(x, axis, mask):
    return lax.ppermute(x, axis, [(i, i ^ mask) for i in range(lax.axis_size(axis))])


def ring(x, axis, step):
    n = lax.axis_size(axis)
    return lax.ppermute(x, axis, [(i, (i + step) % n) for i in range(n)])


def sum_over_tm(send, keep, near, far):
    got = swap(send, "tm", 1)
    away = swap(keep[2:] + got[2:], "tm", 2 * near)
    near_part = swap((keep[1] + got[1]) + away[1], "tm", 2 * far)
    return ((keep[0] + got[0]) + away[0]) + near_part


def sum_over_all(gram):
    core = lax.axis_index("tm") % 2
    n = gram.shape[0] // 2
    mine = lax.dynamic_slice_in_dim(gram, core * n, n, 0)
    other = lax.dynamic_slice_in_dim(gram, (1 - core) * n, n, 0)
    mine = mine + swap(other, "tm", 1)
    for mask in (2, 6):
        mine = mine + swap(mine, "tm", mask)
    for mask in (8, 24, 1, 2, 7):
        mine = mine + swap(mine, "space", mask)
    other = swap(mine, "tm", 1)
    return jnp.where(
        core == 0, jnp.concatenate([mine, other], 0), jnp.concatenate([other, mine], 0)
    )


STEPS = ((1, 3), (3, 1), (1, 3), (3, 1))


def shards(snapshots, sketch, volume, grad_weight, dilation):
    snaps = jnp.transpose(snapshots[:, :, 0, :], (1, 0, 2))
    orders = [(0, far, near, near ^ far) for near, far in STEPS]
    images = sketch_call(snaps, sketch, dilation, grad_weight, orders)
    parts = []
    for n, (near, far) in enumerate(STEPS):
        image = sum_over_tm(images[2 * n], images[2 * n + 1], near, far)
        parts += [image, ring(image, "space", 1), ring(image, "space", -1)]
    panel, gram = panel_call(volume, [FIELDS // len(STEPS)] * len(STEPS), parts)
    gram = sum_over_all(gram)
    basis, upper = basis_call(gram, panel)
    return basis, upper


def solution(mesh):
    return jax.shard_map(
        shards,
        mesh=mesh,
        in_specs=(P("tm", None, "space", None), P("tm", None), P("space", None), P(), P()),
        out_specs=(P("tm", None, "space", None), P()),
        check_vma=False,
    )
```

```python
import functools

import jax
import jax.numpy as jnp
from jax import lax
from jax.experimental import pallas as pl
from jax.experimental.pallas import tpu as pltpu
from jax.sharding import PartitionSpec as P

WX = 16
WY = 16
PLANE = WX * WY
RANK = 256
FIELDS = 12
SHARE = 32
SNAP_DEV = 1024
NZ = 32
ROWS = 98304
HALF = 128
GROUP = 4
DILATIONS = 4
EXACT = lax.Precision.HIGHEST


def hat(offset):
    return jnp.maximum(0.5 - 0.25 * jnp.abs(offset), 0.0)


def hat_slope(source, target, shift):
    ahead = jnp.where(target + shift < 16.0, hat(source - target - shift), 0.0)
    behind = jnp.where(target - shift >= 0.0, hat(source - target + shift), 0.0)
    return 0.5 * (ahead - behind)


def filter_tables(table, blocks):
    lane = lax.broadcasted_iota(jnp.int32, (WX, PLANE), 1)
    px = (lane & 15).astype(jnp.float32)
    py = (lane >> 4).astype(jnp.float32)
    qx = lax.broadcasted_iota(jnp.int32, (WX, PLANE), 0).astype(jnp.float32)
    along_x = hat(px - qx)
    slopes = [hat_slope(px, qx, float(d + 1)) for d in range(DILATIONS)]
    for r, block in enumerate(blocks):
        for h in range(2):
            qy = jnp.full((WX, PLANE), (2 * block + h).astype(jnp.float32))
            rows = pl.ds(32 * r + 16 * h, 16)
            along_y = hat(py - qy)
            table[0, rows, :] = (along_y * along_x).astype(jnp.bfloat16)
            for d in range(DILATIONS):
                mixed = along_y * slopes[d] + hat_slope(py, qy, float(d + 1)) * along_x
                table[d + 1, rows, :] = mixed.astype(jnp.bfloat16)


def split(x):
    high = x.astype(jnp.bfloat16)
    return high, (x - high.astype(jnp.float32)).astype(jnp.bfloat16)


def sketch_kernel(orders, snap_hbm, sketch_hbm, shift_hbm, weight_hbm, *refs):
    outs = refs[: 2 * len(orders)]
    snap, sketch, turned, table, shift, weight, snap_sem, sem = refs[2 * len(orders) :]
    first = [
        pltpu.make_async_copy(sketch_hbm, sketch, sem.at[0]),
        pltpu.make_async_copy(shift_hbm, shift, sem.at[1]),
        pltpu.make_async_copy(weight_hbm, weight, sem.at[2]),
    ]
    copies = [
        pltpu.make_async_copy(snap_hbm.at[f], snap.at[f], snap_sem.at[f]) for f in range(FIELDS)
    ]
    for copy in first + copies:
        copy.start()
    me = lax.axis_index("tm")
    y, core = me // 2, me % 2
    order = orders[0]
    filter_tables(
        table, [2 * (y ^ m) + (1 - core) for m in order] + [2 * (y ^ m) + core for m in order]
    )
    for copy in first:
        copy.wait()
    turned[...] = sketch[...].T
    each = FIELDS // len(orders)
    dot = functools.partial(
        lax.dot_general,
        dimension_numbers=(((1,), (1,)), ((), ())),
        preferred_element_type=jnp.float32,
    )

    def filtered(f, raw):
        high, low = split(raw)
        blur, slope = table[0], table[shift[f]]
        image = (dot(blur, high) + dot(blur, low)) + weight[f] * (
            dot(slope, high) + dot(slope, low)
        )
        n, i = divmod(f, each)
        for r, mask in enumerate(orders[n]):
            at = SHARE * order.index(mask)
            outs[2 * n][r, i] = image[at : at + SHARE]
            outs[2 * n + 1][r, i] = image[HALF + at : HALF + at + SHARE]

    held = None
    for g in range(0, FIELDS + GROUP, GROUP):
        if g < FIELDS:
            for f in range(g, g + GROUP):
                copies[f].wait()
            raws = [
                jnp.dot(turned[...], snap[f], preferred_element_type=jnp.float32)
                for f in range(g, g + GROUP)
            ]
        if held is not None:
            for k in range(GROUP):
                filtered(g - GROUP + k, held[k])
        held = raws


def sketch_call(snaps, sketch, dilation, weight, orders):
    out = jax.ShapeDtypeStruct((4, FIELDS // len(orders), SHARE, RANK), jnp.float32)
    hbm = pl.BlockSpec(memory_space=pltpu.HBM)
    vmem = pl.BlockSpec(memory_space=pltpu.VMEM)
    return pl.pallas_call(
        functools.partial(sketch_kernel, orders),
        in_specs=[hbm] * 4,
        out_specs=[vmem] * (2 * len(orders)),
        out_shape=[out] * (2 * len(orders)),
        scratch_shapes=[
            pltpu.VMEM((FIELDS, SNAP_DEV, PLANE), jnp.bfloat16),
            pltpu.VMEM((SNAP_DEV, RANK), jnp.bfloat16),
            pltpu.VMEM((RANK, SNAP_DEV), jnp.bfloat16),
            pltpu.VMEM((DILATIONS + 1, PLANE, PLANE), jnp.bfloat16),
            pltpu.SMEM((FIELDS,), jnp.int32),
            pltpu.SMEM((FIELDS,), jnp.float32),
            pltpu.SemaphoreType.DMA((FIELDS,)),
            pltpu.SemaphoreType.DMA((3,)),
        ],
        compiler_params=pltpu.CompilerParams(vmem_limit_bytes=49 * 2**20),
    )(snaps, sketch, dilation, weight)


def panel_kernel(counts, volume_ref, *refs):
    parts, (panel_ref, gram_ref) = refs[:-2], refs[-2:]
    me = lax.axis_index("tm")
    row = lax.broadcasted_iota(jnp.int32, (SHARE, PLANE), 0)
    lane = lax.broadcasted_iota(jnp.int32, (SHARE, PLANE), 1)
    volume = jnp.broadcast_to(volume_ref[...], (SHARE, PLANE))
    mine = jnp.sum(jnp.where(lane == row + me * SHARE, volume, 0.0), axis=1, keepdims=True)
    root = jnp.broadcast_to(jnp.sqrt(mine), (SHARE, RANK))
    scaled = []
    at = 0
    for n, count in enumerate(counts):
        here, one, other = parts[3 * n : 3 * n + 3]
        for f in range(count):
            panel = 0.5 * here[f] + 0.25 * (one[f] + other[f])
            panel_ref[at] = panel
            scaled.append(panel * root)
            at += 1
    rows = jnp.concatenate(scaled, axis=0)
    gram = lax.dot_general(
        rows,
        rows,
        (((0,), (0,)), ((), ())),
        precision=EXACT,
        preferred_element_type=jnp.float32,
    )
    gram = gram * (1.0 / ROWS)
    gram_ref[:HALF] = gram[HALF:, :HALF]
    row = lax.broadcasted_iota(jnp.int32, (HALF, HALF), 0)
    lane = lax.broadcasted_iota(jnp.int32, (HALF, HALF), 1)
    last = gram[HALF:, HALF:]
    gram_ref[HALF : 2 * HALF] = jnp.where(row >= lane, gram[:HALF, :HALF], last)
    diag = jnp.sum(jnp.where(row == lane, last, 0.0), axis=0, keepdims=True)
    gram_ref[2 * HALF :] = jnp.broadcast_to(diag, (16, HALF))


def panel_call(volume, counts, parts):
    vmem = pl.BlockSpec(memory_space=pltpu.VMEM)
    return pl.pallas_call(
        functools.partial(panel_kernel, counts),
        in_specs=[vmem] * (1 + len(parts)),
        out_specs=[vmem, vmem],
        out_shape=[
            jax.ShapeDtypeStruct((FIELDS, SHARE, RANK), jnp.float32),
            jax.ShapeDtypeStruct((272, HALF), jnp.float32),
        ],
        compiler_params=pltpu.CompilerParams(vmem_limit_bytes=16 * 2**20),
    )(volume, *parts)


def total(terms):
    terms = list(terms)
    while len(terms) > 1:
        terms = [a + b for a, b in zip(terms[::2], terms[1::2])] + (
            terms[-1:] if len(terms) % 2 else []
        )
    return terms[0]


def factor(rows):
    shape = (8, HALF)
    sub = lax.broadcasted_iota(jnp.int32, shape, 0)
    lane = lax.broadcasted_iota(jnp.int32, shape, 1)
    rows = list(rows)
    count = len(rows)
    uppers, lowers = [], []
    at = [sub == j for j in range(8)]

    def column(x, j):
        return jnp.broadcast_to(x[:, j : j + 1], shape)

    def row_of(x, i):
        return jnp.broadcast_to(x[i : i + 1, :], shape)

    for s in range(count):
        here = rows[s]
        there = jnp.where(lane == sub + 8 * s, 1.0, 0.0)
        inside = (lane >= 8 * s) & (lane < 8 * s + 8)
        cols = [column(here, 8 * s + m) for m in range(8)]
        upper = lower = jnp.zeros(shape, jnp.float32)
        for j in range(0, 8, 2):
            p, q = cols[j], cols[j + 1]
            a, b, c = row_of(p, j), row_of(q, j), row_of(q, j + 1)
            det = a * c - b * b
            inv_det = 1.0 / det
            inv_a = 1.0 / a
            root_a, root_c = lax.rsqrt(a), lax.rsqrt(det * inv_a)
            slope = b * inv_a

            def eliminate(x, kept=None):
                x0, x1 = row_of(x, j), row_of(x, j + 1)
                y0 = (c * x0 - b * x1) * inv_det
                y1 = (a * x1 - b * x0) * inv_det
                new = jnp.where(at[j], y0, jnp.where(at[j + 1], y1, x - p * y0 - q * y1))
                if kept is None:
                    return new
                second = (x1 - slope * x0) * root_c
                return new, jnp.where(at[j], x0 * root_a, jnp.where(at[j + 1], second, kept))

            here, upper = eliminate(here, upper)
            there, lower = eliminate(there, lower)
            for m in range(j + 2, 8):
                cols[m] = eliminate(cols[m])
        uppers.append(jnp.where(lane >= sub + 8 * s, upper, 0.0))
        lowers.append(jnp.where(inside, lower, jnp.where(lane < 8 * s, upper, 0.0)))
        if s + 1 == count:
            break
        solved = jnp.where(inside, there, here)
        solved_rows = [row_of(solved, m) for m in range(8)]
        for t in range(s + 1, count):
            weights = [column(rows[t], 8 * s + m) for m in range(8)]
            rows[t] = jnp.where(inside, 0.0, rows[t]) - total(
                weights[m] * solved_rows[m] for m in range(8)
            )
    return uppers, lowers


def basis_kernel(gram_ref, panel_ref, basis_ref, upper_ref):
    row = lax.broadcasted_iota(jnp.int32, (HALF, HALF), 0)
    lane = lax.broadcasted_iota(jnp.int32, (HALF, HALF), 1)
    cross = gram_ref[:HALF]
    mixed = gram_ref[HALF : 2 * HALF]
    turned = mixed.T
    first = jnp.where(row >= lane, mixed, turned)
    diag = jnp.broadcast_to(gram_ref[2 * HALF : 2 * HALF + 1, :], (HALF, HALF))
    last = jnp.where(row < lane, mixed, jnp.where(row > lane, turned, diag))
    cells = FIELDS * SHARE

    def dot(a, b, da, db):
        return lax.dot_general(
            a,
            b,
            (((da,), (db,)), ((), ())),
            precision=EXACT,
            preferred_element_type=jnp.float32,
        )

    def put(x, h):
        for f in range(FIELDS):
            basis_ref[pl.ds(2 * f + h, SHARE, stride=2 * FIELDS), :] = x[
                SHARE * f : SHARE * f + SHARE
            ]

    groups = range(HALF // 8)
    uppers, lowers = factor([first[8 * t : 8 * t + 8] for t in groups])
    low_a = jnp.concatenate(lowers, axis=0)
    upper_ref[:HALF, :HALF] = jnp.concatenate(uppers, axis=0)
    side = dot(low_a, cross, 1, 1)
    last = last - dot(side, side, 0, 0)
    upper_ref[:HALF, HALF:] = side
    upper_ref[HALF:, :HALF] = jnp.zeros((HALF, HALF), jnp.float32)
    basis_a = dot(panel_ref[:, :, :HALF].reshape(cells, HALF), low_a, 1, 1)
    rest = panel_ref[:, :, HALF:].reshape(cells, HALF) - dot(basis_a, side, 1, 0)
    put(basis_a, 0)
    uppers, lowers = factor([last[8 * t : 8 * t + 8] for t in groups])
    low_b = jnp.concatenate(lowers, axis=0)
    upper_ref[HALF:, HALF:] = jnp.concatenate(uppers, axis=0)
    put(dot(rest, low_b, 1, 1), 1)


def basis_call(gram, panel):
    vmem = pl.BlockSpec(memory_space=pltpu.VMEM)
    basis, upper = pl.pallas_call(
        basis_kernel,
        in_specs=[vmem, vmem],
        out_specs=[vmem, vmem],
        out_shape=[
            jax.ShapeDtypeStruct((SHARE * FIELDS * 2, HALF), jnp.float32),
            jax.ShapeDtypeStruct((RANK, RANK), jnp.float32),
        ],
        compiler_params=pltpu.CompilerParams(vmem_limit_bytes=32 * 2**20),
    )(gram, panel)
    return basis.reshape(SHARE, FIELDS, 1, RANK), upper


def swap(x, axis, mask):
    return lax.ppermute(x, axis, [(i, i ^ mask) for i in range(lax.axis_size(axis))])


def swap_next(x):
    n = lax.axis_size("space")
    pairs = [(i, i + 1) for i in range(1, n - 1, 2)]
    return lax.ppermute(x, "space", pairs + [(j, i) for i, j in pairs])


def sum_over_tm(send, keep, near, far):
    mine = keep + swap(send, "tm", 1)
    mine = mine[:2] + swap(mine[2:], "tm", 2 * near)
    return mine[0] + swap(mine[1], "tm", 2 * far)


def parity(y, x, z):
    return (y ^ x ^ z ^ (z >> 1)) & 1


def span(masks):
    out = []
    for picks in range(1, 2 ** len(masks)):
        mask = (0, 0, 0)
        for i, part in enumerate(masks):
            if picks >> i & 1:
                mask = tuple(a ^ b for a, b in zip(mask, part))
        out.append(mask)
    return out


def sum_over_all(gram):
    tm, space = lax.axis_index("tm"), lax.axis_index("space")
    side = (tm & 1) ^ parity(tm >> 1, space >> 3, space & 7)
    n = gram.shape[0] // 2
    mine = lax.dynamic_slice_in_dim(gram, side * n, n, 0)
    other = lax.dynamic_slice_in_dim(gram, (1 - side) * n, n, 0)
    mine = mine + swap(other, "tm", 1)
    for masks in GRAM_STEPS:
        parts = []
        for y, x, z in span(masks):
            flip = (2 * y + parity(y, x, z)) * NZ + 8 * x + z
            parts.append(swap(mine, ("tm", "space"), flip))
        mine = mine + functools.reduce(jnp.add, parts)
    other = swap(mine, "tm", 1)
    return jnp.where(
        side == 0, jnp.concatenate([mine, other], 0), jnp.concatenate([other, mine], 0)
    )


STEPS = ((1, 3), (3, 1), (1, 3), (3, 1))
JOIN = 2
GRAM_STEPS = (
    ((1, 0, 0), (0, 1, 0)),
    ((3, 0, 0), (0, 3, 0)),
    ((0, 0, 1), (0, 0, 2)),
    ((0, 0, 6),),
)


def shards(snapshots, sketch, volume, grad_weight, dilation):
    snaps = jnp.transpose(snapshots[:, :, 0, :], (1, 0, 2))
    orders = [(0, far, near, near ^ far) for near, far in STEPS]
    images = sketch_call(snaps, sketch, dilation, grad_weight, orders)
    summed = [
        sum_over_tm(images[2 * n], images[2 * n + 1], near, far)
        for n, (near, far) in enumerate(STEPS)
    ]
    parts = []
    for n in range(0, len(summed), JOIN):
        image = jnp.concatenate(summed[n : n + JOIN], 0)
        parts += [image, swap(image, "space", 1), swap_next(image)]
    panel, gram = panel_call(volume, [p.shape[0] for p in parts[::3]], parts)
    gram = sum_over_all(gram)
    basis, upper = basis_call(gram, panel)
    return basis, upper


def solution(mesh):
    return jax.shard_map(
        shards,
        mesh=mesh,
        in_specs=(P("tm", None, "space", None), P("tm", None), P("space", None), P(), P()),
        out_specs=(P("tm", None, "space", None), P()),
        check_vma=False,
    )
```

```python
import functools

import jax
import jax.numpy as jnp
from jax import lax
from jax.experimental import pallas as pl
from jax.experimental.pallas import tpu as pltpu
from jax.sharding import PartitionSpec as P

WX = 16
WY = 16
PLANE = WX * WY
RANK = 256
FIELDS = 12
SHARE = 32
SNAP_DEV = 1024
NZ = 32
ROWS = 98304
HALF = 128
GROUP = 3
DILATIONS = 4
EXACT = lax.Precision.HIGHEST


def hat(offset):
    return jnp.maximum(0.5 - 0.25 * jnp.abs(offset), 0.0)


def hat_slope(source, target, shift):
    ahead = jnp.where(target + shift < 16.0, hat(source - target - shift), 0.0)
    behind = jnp.where(target - shift >= 0.0, hat(source - target + shift), 0.0)
    return 0.5 * (ahead - behind)


def filter_tables(table, blocks):
    lane = lax.broadcasted_iota(jnp.int32, (WX, PLANE), 1)
    px = (lane & 15).astype(jnp.float32)
    py = (lane >> 4).astype(jnp.float32)
    qx = lax.broadcasted_iota(jnp.int32, (WX, PLANE), 0).astype(jnp.float32)
    along_x = hat(px - qx)
    slopes = [hat_slope(px, qx, float(d + 1)) for d in range(DILATIONS)]
    for r, block in enumerate(blocks):
        for h in range(2):
            qy = jnp.full((WX, PLANE), (2 * block + h).astype(jnp.float32))
            rows = pl.ds(32 * r + 16 * h, 16)
            along_y = hat(py - qy)
            table[0, rows, :] = (along_y * along_x).astype(jnp.bfloat16)
            for d in range(DILATIONS):
                mixed = along_y * slopes[d] + hat_slope(py, qy, float(d + 1)) * along_x
                table[d + 1, rows, :] = mixed.astype(jnp.bfloat16)


def step_masks(core):
    return 1 + 2 * core, 3 - 2 * core


def step_order(core):
    near, far = step_masks(core)
    return 0, far, near, near ^ far


def split(x):
    high = x.astype(jnp.bfloat16)
    return high, (x - high.astype(jnp.float32)).astype(jnp.bfloat16)


def sketch_kernel(first, count, snap_hbm, sketch_hbm, shift_hbm, weight_hbm, *refs):
    send_ref, keep_ref, snap, sketch, turned, table, shift, weight, snap_sem, sem = refs
    heads = [
        pltpu.make_async_copy(sketch_hbm, sketch, sem.at[0]),
        pltpu.make_async_copy(shift_hbm, shift, sem.at[1]),
        pltpu.make_async_copy(weight_hbm, weight, sem.at[2]),
    ]
    copies = [
        pltpu.make_async_copy(snap_hbm.at[first + f], snap.at[f], snap_sem.at[f])
        for f in range(count)
    ]
    for copy in heads + copies:
        copy.start()
    me = lax.axis_index("tm")
    y, core = me // 2, me % 2
    other = 1 - core
    filter_tables(
        table,
        [2 * (y ^ m) + other for m in step_order(other)]
        + [2 * (y ^ m) + core for m in step_order(core)],
    )
    for copy in heads:
        copy.wait()
    turned[...] = sketch[...].T
    dot = functools.partial(
        lax.dot_general,
        dimension_numbers=(((1,), (1,)), ((), ())),
        preferred_element_type=jnp.float32,
    )

    def filtered(f, raw):
        high, low = split(raw)
        blur, slope = table[0], table[shift[first + f]]
        image = (dot(blur, high) + dot(blur, low)) + weight[first + f] * (
            dot(slope, high) + dot(slope, low)
        )
        send_ref[:, f] = image[:HALF].reshape(4, SHARE, RANK)
        keep_ref[:, f] = image[HALF:].reshape(4, SHARE, RANK)

    held = None
    for g in range(0, count + GROUP, GROUP):
        if g < count:
            for f in range(g, g + GROUP):
                copies[f].wait()
            raws = [
                jnp.dot(turned[...], snap[f], preferred_element_type=jnp.float32)
                for f in range(g, g + GROUP)
            ]
        if held is not None:
            for k in range(GROUP):
                filtered(g - GROUP + k, held[k])
        held = raws


def sketch_call(snaps, sketch, dilation, weight, first, count):
    out = jax.ShapeDtypeStruct((4, count, SHARE, RANK), jnp.float32)
    hbm = pl.BlockSpec(memory_space=pltpu.HBM)
    vmem = pl.BlockSpec(memory_space=pltpu.VMEM)
    return pl.pallas_call(
        functools.partial(sketch_kernel, first, count),
        in_specs=[hbm] * 4,
        out_specs=[vmem] * 2,
        out_shape=[out] * 2,
        scratch_shapes=[
            pltpu.VMEM((count, SNAP_DEV, PLANE), jnp.bfloat16),
            pltpu.VMEM((SNAP_DEV, RANK), jnp.bfloat16),
            pltpu.VMEM((RANK, SNAP_DEV), jnp.bfloat16),
            pltpu.VMEM((DILATIONS + 1, PLANE, PLANE), jnp.bfloat16),
            pltpu.SMEM((FIELDS,), jnp.int32),
            pltpu.SMEM((FIELDS,), jnp.float32),
            pltpu.SemaphoreType.DMA((count,)),
            pltpu.SemaphoreType.DMA((3,)),
        ],
        compiler_params=pltpu.CompilerParams(vmem_limit_bytes=50 * 2**20),
        cost_estimate=pl.CostEstimate(
            flops=count * 2**28, bytes_accessed=count * 2**20, transcendentals=0
        ),
    )(snaps, sketch, dilation, weight)


def panel_kernel(counts, volume_ref, *refs):
    parts, (panel_ref, gram_ref) = refs[:-2], refs[-2:]
    me, plane = lax.axis_index("tm"), lax.axis_index("space")
    inner = (plane > 0) & (plane < NZ - 1)
    use_first, use_second = inner | (me % 2 == 0), inner | (me % 2 == 1)
    row = lax.broadcasted_iota(jnp.int32, (SHARE, PLANE), 0)
    lane = lax.broadcasted_iota(jnp.int32, (SHARE, PLANE), 1)
    volume = jnp.broadcast_to(volume_ref[...], (SHARE, PLANE))
    mine = jnp.sum(jnp.where(lane == row + me * SHARE, volume, 0.0), axis=1, keepdims=True)
    root = jnp.broadcast_to(jnp.sqrt(mine), (SHARE, RANK))
    scaled = []
    at = 0
    for n, count in enumerate(counts):
        here, first, second = parts[3 * n : 3 * n + 3]
        for f in range(count):
            panel = 0.5 * here[f]
            panel = panel + jnp.where(use_first, 0.25 * first[f], 0.0)
            panel = panel + jnp.where(use_second, 0.25 * second[f], 0.0)
            panel_ref[at] = panel
            scaled.append(panel * root)
            at += 1
    rows = jnp.concatenate(scaled, axis=0)
    gram = lax.dot_general(
        rows,
        rows,
        (((0,), (0,)), ((), ())),
        precision=EXACT,
        preferred_element_type=jnp.float32,
    )
    gram = gram * (1.0 / ROWS)
    gram_ref[:HALF] = gram[HALF:, :HALF]
    row = lax.broadcasted_iota(jnp.int32, (HALF, HALF), 0)
    lane = lax.broadcasted_iota(jnp.int32, (HALF, HALF), 1)
    last = gram[HALF:, HALF:]
    gram_ref[HALF : 2 * HALF] = jnp.where(row >= lane, gram[:HALF, :HALF], last)
    diag = jnp.sum(jnp.where(row == lane, last, 0.0), axis=0, keepdims=True)
    gram_ref[2 * HALF :] = jnp.broadcast_to(diag, (16, HALF))


def panel_call(volume, counts, parts):
    vmem = pl.BlockSpec(memory_space=pltpu.VMEM)
    return pl.pallas_call(
        functools.partial(panel_kernel, counts),
        in_specs=[vmem] * (1 + len(parts)),
        out_specs=[vmem, vmem],
        out_shape=[
            jax.ShapeDtypeStruct((FIELDS, SHARE, RANK), jnp.float32),
            jax.ShapeDtypeStruct((272, HALF), jnp.float32),
        ],
        compiler_params=pltpu.CompilerParams(vmem_limit_bytes=16 * 2**20),
    )(volume, *parts)


def total(terms):
    terms = list(terms)
    while len(terms) > 1:
        terms = [a + b for a, b in zip(terms[::2], terms[1::2])] + (
            terms[-1:] if len(terms) % 2 else []
        )
    return terms[0]


def factor(rows):
    shape = (8, HALF)
    sub = lax.broadcasted_iota(jnp.int32, shape, 0)
    lane = lax.broadcasted_iota(jnp.int32, shape, 1)
    rows = list(rows)
    count = len(rows)
    uppers, lowers = [], []
    at = [sub == j for j in range(8)]

    def column(x, j):
        return jnp.broadcast_to(x[:, j : j + 1], shape)

    def row_of(x, i):
        return jnp.broadcast_to(x[i : i + 1, :], shape)

    cols = [column(rows[0], m) for m in range(8)]
    for s in range(count):
        here = rows[s]
        there = jnp.where(lane == sub + 8 * s, 1.0, 0.0)
        inside = (lane >= 8 * s) & (lane < 8 * s + 8)
        last = s + 1 == count
        ahead = [] if last else [column(here, 8 * s + 8 + m) for m in range(8)]
        upper = lower = jnp.zeros(shape, jnp.float32)
        for j in range(0, 8, 2):
            p, q = cols[j], cols[j + 1]
            a, b, c = row_of(p, j), row_of(q, j), row_of(q, j + 1)
            det = a * c - b * b
            inv_det = 1.0 / det
            inv_a = 1.0 / a
            root_a, root_c = lax.rsqrt(a), lax.rsqrt(det * inv_a)
            slope = b * inv_a
            into_a, into_b, into_c = a * inv_det, b * inv_det, c * inv_det

            def eliminate(x):
                x0, x1 = row_of(x, j), row_of(x, j + 1)
                y0 = into_c * x0 - into_b * x1
                y1 = into_a * x1 - into_b * x0
                return jnp.where(at[j], y0, jnp.where(at[j + 1], y1, x - p * y0 - q * y1))

            def factored(x, kept):
                x0, x1 = row_of(x, j), row_of(x, j + 1)
                second = (x1 - slope * x0) * root_c
                return jnp.where(at[j], x0 * root_a, jnp.where(at[j + 1], second, kept))

            upper, lower = factored(here, upper), factored(there, lower)
            here, there = eliminate(here), eliminate(there)
            for m in range(j + 2, 8):
                cols[m] = eliminate(cols[m])
            ahead = [eliminate(x) for x in ahead]
        uppers.append(jnp.where(lane >= sub + 8 * s, upper, 0.0))
        lowers.append(jnp.where(inside, lower, jnp.where(lane < 8 * s, upper, 0.0)))
        if last:
            break
        weights = [column(rows[s + 1], 8 * s + m) for m in range(8)]
        cols = [
            column(rows[s + 1], 8 * s + 8 + m)
            - total(weights[k] * row_of(ahead[m], k) for k in range(8))
            for m in range(8)
        ]
        solved = jnp.where(inside, there, here)
        solved_rows = [row_of(solved, m) for m in range(8)]
        for t in range(s + 1, count):
            if t > s + 1:
                weights = [column(rows[t], 8 * s + m) for m in range(8)]
            rows[t] = jnp.where(inside, 0.0, rows[t]) - total(
                weights[m] * solved_rows[m] for m in range(8)
            )
    return uppers, lowers


def basis_kernel(gram_ref, panel_ref, basis_ref, upper_ref):
    row = lax.broadcasted_iota(jnp.int32, (HALF, HALF), 0)
    lane = lax.broadcasted_iota(jnp.int32, (HALF, HALF), 1)
    cross = gram_ref[:HALF]
    mixed = gram_ref[HALF : 2 * HALF]
    turned = mixed.T
    first = jnp.where(row >= lane, mixed, turned)
    diag = jnp.broadcast_to(gram_ref[2 * HALF : 2 * HALF + 1, :], (HALF, HALF))
    last = jnp.where(row < lane, mixed, jnp.where(row > lane, turned, diag))
    cells = FIELDS * SHARE

    def dot(a, b, da, db):
        return lax.dot_general(
            a,
            b,
            (((da,), (db,)), ((), ())),
            precision=EXACT,
            preferred_element_type=jnp.float32,
        )

    def put(x, h):
        for f in range(FIELDS):
            basis_ref[pl.ds(2 * f + h, SHARE, stride=2 * FIELDS), :] = x[
                SHARE * f : SHARE * f + SHARE
            ]

    groups = range(HALF // 8)
    uppers, lowers = factor([first[8 * t : 8 * t + 8] for t in groups])
    low_a = jnp.concatenate(lowers, axis=0)
    upper_ref[:HALF, :HALF] = jnp.concatenate(uppers, axis=0)
    side = dot(low_a, cross, 1, 1)
    last = last - dot(side, side, 0, 0)
    upper_ref[:HALF, HALF:] = side
    upper_ref[HALF:, :HALF] = jnp.zeros((HALF, HALF), jnp.float32)
    basis_a = dot(panel_ref[:, :, :HALF].reshape(cells, HALF), low_a, 1, 1)
    rest = panel_ref[:, :, HALF:].reshape(cells, HALF) - dot(basis_a, side, 1, 0)
    put(basis_a, 0)
    uppers, lowers = factor([last[8 * t : 8 * t + 8] for t in groups])
    low_b = jnp.concatenate(lowers, axis=0)
    upper_ref[HALF:, HALF:] = jnp.concatenate(uppers, axis=0)
    put(dot(rest, low_b, 1, 1), 1)


def basis_call(gram, panel):
    vmem = pl.BlockSpec(memory_space=pltpu.VMEM)
    basis, upper = pl.pallas_call(
        basis_kernel,
        in_specs=[vmem, vmem],
        out_specs=[vmem, vmem],
        out_shape=[
            jax.ShapeDtypeStruct((SHARE * FIELDS * 2, HALF), jnp.float32),
            jax.ShapeDtypeStruct((RANK, RANK), jnp.float32),
        ],
        compiler_params=pltpu.CompilerParams(vmem_limit_bytes=32 * 2**20),
    )(gram, panel)
    return basis.reshape(SHARE, FIELDS, 1, RANK), upper


def swap(x, axis, mask):
    return lax.ppermute(x, axis, [(i, i ^ mask) for i in range(lax.axis_size(axis))])


def permute(x, target):
    pairs = []
    for source in range(2 * 4 * NZ):
        tm, space = divmod(source, NZ)
        y, core, gx, gz = target(tm >> 1, tm & 1, space >> 3, space & 7)
        pairs.append((source, (2 * y + core) * NZ + 8 * gx + gz))
    return lax.ppermute(x, ("tm", "space"), pairs)


def step_swap(x, which):
    return permute(x, lambda y, c, gx, gz: (y ^ step_masks(c)[which], c, gx, gz))


def halo_swap(x, which):
    def target(y, c, gx, gz):
        plane = 8 * gx + gz
        if c == which:
            goal = plane ^ 1
        else:
            goal = plane + 1 if plane & 1 else plane - 1
        return (y, c, goal >> 3, goal & 7) if 0 <= goal < NZ else (y ^ 1, c, gx, gz)

    return permute(x, target)


def sum_along_y(mine):
    mine = mine[:2] + step_swap(mine[2:], 0)
    return mine[0] + step_swap(mine[1], 1)


def parity(y, x, z):
    return (y ^ x ^ z ^ (z >> 1)) & 1


def gram_swap(x, masks):
    def target(y, c, gx, gz):
        dy, dx, dz = masks[c ^ parity(y, gx, gz)]
        return y ^ dy, c ^ parity(dy, dx, dz), gx ^ dx, gz ^ dz

    return permute(x, target)


def sum_over_all(gram):
    tm, space = lax.axis_index("tm"), lax.axis_index("space")
    side = (tm & 1) ^ parity(tm >> 1, space >> 3, space & 7)
    n = gram.shape[0] // 2
    mine = lax.dynamic_slice_in_dim(gram, side * n, n, 0)
    other = lax.dynamic_slice_in_dim(gram, (1 - side) * n, n, 0)
    mine = mine + swap(other, "tm", 1)
    for step in GRAM_STEPS:
        mine = mine + functools.reduce(jnp.add, [gram_swap(mine, masks) for masks in step])
    other = swap(mine, "tm", 1)
    return jnp.where(
        side == 0, jnp.concatenate([mine, other], 0), jnp.concatenate([other, mine], 0)
    )


PARTS = ((0, 6), (6, 6))
def single(a, b):
    return ((a, b),)


def four(a, b):
    both = [tuple(i ^ j for i, j in zip(*pair)) for pair in (a, b)]
    return (a[0], b[0]), (a[1], b[1]), (both[0], both[1])


Y1, Y3 = (1, 0, 0), (3, 0, 0)
X1, X3 = (0, 1, 0), (0, 3, 0)
Z1, Z2, Z6 = (0, 0, 1), (0, 0, 2), (0, 0, 6)
GRAM_STEPS = (
    single(Y3, Z6),
    single(X3, Y3),
    single(Z6, X3),
    four((Y1, X1), (Z1, Z2)),
    four((Z1, Z2), (Y1, X1)),
)


def shards(snapshots, sketch, volume, grad_weight, dilation):
    snaps = jnp.transpose(snapshots[:, :, 0, :], (1, 0, 2))
    parts = []
    for first, count in PARTS:
        send, keep = sketch_call(snaps, sketch, dilation, grad_weight, first, count)
        image = sum_along_y(keep + swap(send, "tm", 1))
        parts += [image, halo_swap(image, 0), halo_swap(image, 1)]
    panel, gram = panel_call(volume, [p.shape[0] for p in parts[::3]], parts)
    gram = sum_over_all(gram)
    basis, upper = basis_call(gram, panel)
    return basis, upper


def solution(mesh):
    return jax.shard_map(
        shards,
        mesh=mesh,
        in_specs=(P("tm", None, "space", None), P("tm", None), P("space", None), P(), P()),
        out_specs=(P("tm", None, "space", None), P()),
        check_vma=False,
    )
```

```python
import functools

import jax
import jax.numpy as jnp
from jax import lax
from jax.experimental import pallas as pl
from jax.experimental.pallas import tpu as pltpu
from jax.sharding import PartitionSpec as P

WX = 16
WY = 16
PLANE = WX * WY
RANK = 256
FIELDS = 12
SHARE = 32
SNAP_DEV = 1024
NZ = 32
ROWS = 98304
HALF = 128
GROUP = 3
DILATIONS = 4
EXACT = lax.Precision.HIGHEST


def hat(offset):
    return jnp.maximum(0.5 - 0.25 * jnp.abs(offset), 0.0)


def hat_slope(source, target, shift):
    ahead = jnp.where(target + shift < 16.0, hat(source - target - shift), 0.0)
    behind = jnp.where(target - shift >= 0.0, hat(source - target + shift), 0.0)
    return 0.5 * (ahead - behind)


def filter_tables(table, blocks):
    lane = lax.broadcasted_iota(jnp.int32, (WX, PLANE), 1)
    px = (lane & 15).astype(jnp.float32)
    py = (lane >> 4).astype(jnp.float32)
    qx = lax.broadcasted_iota(jnp.int32, (WX, PLANE), 0).astype(jnp.float32)
    along_x = hat(px - qx)
    slopes = [hat_slope(px, qx, float(d + 1)) for d in range(DILATIONS)]
    for r, block in enumerate(blocks):
        for h in range(2):
            qy = jnp.full((WX, PLANE), (2 * block + h).astype(jnp.float32))
            rows = pl.ds(32 * r + 16 * h, 16)
            along_y = hat(py - qy)
            table[0, rows, :] = (along_y * along_x).astype(jnp.bfloat16)
            for d in range(DILATIONS):
                mixed = along_y * slopes[d] + hat_slope(py, qy, float(d + 1)) * along_x
                table[d + 1, rows, :] = mixed.astype(jnp.bfloat16)


def step_masks(side):
    return 1 + 2 * side, 3 - 2 * side


def step_blocks(y, core):
    near, far = step_masks(core ^ (y & 1))
    return [2 * (y ^ m) + (core ^ (m & 1)) for m in (0, far, near, near ^ far)]


def split(x):
    high = x.astype(jnp.bfloat16)
    return high, (x - high.astype(jnp.float32)).astype(jnp.bfloat16)


def sketch_kernel(first, count, later, snap_ref, sketch_hbm, shift_hbm, weight_hbm, *refs):
    held_refs = refs[2 : 2 + (later > 0)]
    send_ref, keep_ref = refs[:2]
    snap, sketch, turned, table, shift, weight, snap_sem, sem = refs[2 + (later > 0) :]
    heads = [
        pltpu.make_async_copy(sketch_hbm, sketch, sem.at[0]),
        pltpu.make_async_copy(shift_hbm, shift, sem.at[1]),
        pltpu.make_async_copy(weight_hbm, weight, sem.at[2]),
    ]
    copies = []
    if later:
        places = [snap.at[f] for f in range(count)] + [held_refs[0].at[f] for f in range(later)]
        copies = [
            pltpu.make_async_copy(snap_ref.at[f], place, snap_sem.at[f])
            for f, place in enumerate(places)
        ]
    else:
        snap = snap_ref
    for copy in heads + copies:
        copy.start()
    me = lax.axis_index("tm")
    y, core = me // 2, me % 2
    filter_tables(table, step_blocks(y, 1 - core) + step_blocks(y, core))
    for copy in heads:
        copy.wait()
    turned[...] = sketch[...].T
    dot = functools.partial(
        lax.dot_general,
        dimension_numbers=(((1,), (1,)), ((), ())),
        preferred_element_type=jnp.float32,
    )

    def filtered(f, raw):
        high, low = split(raw)
        blur, slope = table[0], table[shift[first + f]]
        image = (dot(blur, high) + dot(blur, low)) + weight[first + f] * (
            dot(slope, high) + dot(slope, low)
        )
        send_ref[:, f] = image[:HALF].reshape(4, SHARE, RANK)
        keep_ref[:, f] = image[HALF:].reshape(4, SHARE, RANK)

    held = None
    for g in range(0, count + GROUP, GROUP):
        if g < count:
            for copy in copies[g : g + GROUP]:
                copy.wait()
            raws = [
                jnp.dot(turned[...], snap[f], preferred_element_type=jnp.float32)
                for f in range(g, g + GROUP)
            ]
        if held is not None:
            for k in range(GROUP):
                filtered(g - GROUP + k, held[k])
        held = raws
    for copy in copies[count:]:
        copy.wait()


def sketch_call(snaps, sketch, dilation, weight, first, count, later):
    out = jax.ShapeDtypeStruct((4, count, SHARE, RANK), jnp.float32)
    hbm = pl.BlockSpec(memory_space=pltpu.HBM)
    vmem = pl.BlockSpec(memory_space=pltpu.VMEM)
    rest = [jax.ShapeDtypeStruct((later, SNAP_DEV, PLANE), jnp.bfloat16)] if later else []
    return pl.pallas_call(
        functools.partial(sketch_kernel, first, count, later),
        in_specs=[hbm if later else vmem] + [hbm] * 3,
        out_specs=[vmem] * (2 + len(rest)),
        out_shape=[out] * 2 + rest,
        scratch_shapes=[
            pltpu.VMEM((count if later else 1, SNAP_DEV, PLANE), jnp.bfloat16),
            pltpu.VMEM((SNAP_DEV, RANK), jnp.bfloat16),
            pltpu.VMEM((RANK, SNAP_DEV), jnp.bfloat16),
            pltpu.VMEM((DILATIONS + 1, PLANE, PLANE), jnp.bfloat16),
            pltpu.SMEM((FIELDS,), jnp.int32),
            pltpu.SMEM((FIELDS,), jnp.float32),
            pltpu.SemaphoreType.DMA((count + later,)),
            pltpu.SemaphoreType.DMA((3,)),
        ],
        compiler_params=pltpu.CompilerParams(vmem_limit_bytes=46 * 2**20),
        cost_estimate=pl.CostEstimate(
            flops=count * 2**28, bytes_accessed=count * 2**20, transcendentals=0
        ),
    )(snaps, sketch, dilation, weight)


def panel_kernel(counts, volume_ref, *refs):
    parts, (panel_ref, gram_ref) = refs[:-2], refs[-2:]
    me, plane = lax.axis_index("tm"), lax.axis_index("space")
    inner = (plane > 0) & (plane < NZ - 1)
    use_first, use_second = inner | (me % 2 == 0), inner | (me % 2 == 1)
    row = lax.broadcasted_iota(jnp.int32, (SHARE, PLANE), 0)
    lane = lax.broadcasted_iota(jnp.int32, (SHARE, PLANE), 1)
    volume = jnp.broadcast_to(volume_ref[...], (SHARE, PLANE))
    mine = jnp.sum(jnp.where(lane == row + me * SHARE, volume, 0.0), axis=1, keepdims=True)
    root = jnp.broadcast_to(jnp.sqrt(mine), (SHARE, RANK))
    scaled = []
    at = 0
    for n, count in enumerate(counts):
        here, first, second = parts[3 * n : 3 * n + 3]
        for f in range(count):
            panel = 0.5 * here[f]
            panel = panel + jnp.where(use_first, 0.25 * first[f], 0.0)
            panel = panel + jnp.where(use_second, 0.25 * second[f], 0.0)
            panel_ref[at] = panel
            scaled.append(panel * root)
            at += 1
    rows = jnp.concatenate(scaled, axis=0)
    gram = lax.dot_general(
        rows,
        rows,
        (((0,), (0,)), ((), ())),
        precision=EXACT,
        preferred_element_type=jnp.float32,
    )
    gram = gram * (1.0 / ROWS)
    gram_ref[:HALF] = gram[HALF:, :HALF]
    row = lax.broadcasted_iota(jnp.int32, (HALF, HALF), 0)
    lane = lax.broadcasted_iota(jnp.int32, (HALF, HALF), 1)
    last = gram[HALF:, HALF:]
    gram_ref[HALF : 2 * HALF] = jnp.where(row >= lane, gram[:HALF, :HALF], last)
    diag = jnp.sum(jnp.where(row == lane, last, 0.0), axis=0, keepdims=True)
    gram_ref[2 * HALF :] = jnp.broadcast_to(diag, (16, HALF))


def panel_call(volume, counts, parts):
    vmem = pl.BlockSpec(memory_space=pltpu.VMEM)
    return pl.pallas_call(
        functools.partial(panel_kernel, counts),
        in_specs=[vmem] * (1 + len(parts)),
        out_specs=[vmem, vmem],
        out_shape=[
            jax.ShapeDtypeStruct((FIELDS, SHARE, RANK), jnp.float32),
            jax.ShapeDtypeStruct((272, HALF), jnp.float32),
        ],
        compiler_params=pltpu.CompilerParams(vmem_limit_bytes=16 * 2**20),
    )(volume, *parts)


def total(terms):
    terms = list(terms)
    while len(terms) > 1:
        terms = [a + b for a, b in zip(terms[::2], terms[1::2])] + (
            terms[-1:] if len(terms) % 2 else []
        )
    return terms[0]


def factor(rows):
    shape = (8, HALF)
    sub = lax.broadcasted_iota(jnp.int32, shape, 0)
    lane = lax.broadcasted_iota(jnp.int32, shape, 1)
    rows = list(rows)
    count = len(rows)
    uppers, lowers = [], []
    at = [sub == j for j in range(8)]

    def column(x, j):
        return jnp.broadcast_to(x[:, j : j + 1], shape)

    def row_of(x, i):
        return jnp.broadcast_to(x[i : i + 1, :], shape)

    cols = [column(rows[0], m) for m in range(8)]
    for s in range(count):
        here = rows[s]
        there = jnp.where(lane == sub + 8 * s, 1.0, 0.0)
        inside = (lane >= 8 * s) & (lane < 8 * s + 8)
        last = s + 1 == count
        ahead = [] if last else [column(here, 8 * s + 8 + m) for m in range(8)]
        upper = lower = jnp.zeros(shape, jnp.float32)
        for j in range(0, 8, 2):
            p, q = cols[j], cols[j + 1]
            a, b, c = row_of(p, j), row_of(q, j), row_of(q, j + 1)
            det = a * c - b * b
            inv_det = 1.0 / det
            inv_a = 1.0 / a
            root_a, root_c = lax.rsqrt(a), lax.rsqrt(det * inv_a)
            slope = b * inv_a
            into_a, into_b, into_c = a * inv_det, b * inv_det, c * inv_det

            def eliminate(x):
                x0, x1 = row_of(x, j), row_of(x, j + 1)
                y0 = into_c * x0 - into_b * x1
                y1 = into_a * x1 - into_b * x0
                return jnp.where(at[j], y0, jnp.where(at[j + 1], y1, x - p * y0 - q * y1))

            def factored(x, kept):
                x0, x1 = row_of(x, j), row_of(x, j + 1)
                second = (x1 - slope * x0) * root_c
                return jnp.where(at[j], x0 * root_a, jnp.where(at[j + 1], second, kept))

            upper, lower = factored(here, upper), factored(there, lower)
            here, there = eliminate(here), eliminate(there)
            for m in range(j + 2, 8):
                cols[m] = eliminate(cols[m])
            ahead = [eliminate(x) for x in ahead]
        uppers.append(jnp.where(lane >= sub + 8 * s, upper, 0.0))
        lowers.append(jnp.where(inside, lower, jnp.where(lane < 8 * s, upper, 0.0)))
        if last:
            break
        weights = [column(rows[s + 1], 8 * s + m) for m in range(8)]
        cols = [
            column(rows[s + 1], 8 * s + 8 + m)
            - total(weights[k] * row_of(ahead[m], k) for k in range(8))
            for m in range(8)
        ]
        solved = jnp.where(inside, there, here)
        solved_rows = [row_of(solved, m) for m in range(8)]
        for t in range(s + 1, count):
            if t > s + 1:
                weights = [column(rows[t], 8 * s + m) for m in range(8)]
            rows[t] = jnp.where(inside, 0.0, rows[t]) - total(
                weights[m] * solved_rows[m] for m in range(8)
            )
    return uppers, lowers


def basis_kernel(gram_ref, panel_ref, basis_ref, upper_ref):
    row = lax.broadcasted_iota(jnp.int32, (HALF, HALF), 0)
    lane = lax.broadcasted_iota(jnp.int32, (HALF, HALF), 1)
    cross = gram_ref[:HALF]
    mixed = gram_ref[HALF : 2 * HALF]
    turned = mixed.T
    first = jnp.where(row >= lane, mixed, turned)
    diag = jnp.broadcast_to(gram_ref[2 * HALF : 2 * HALF + 1, :], (HALF, HALF))
    last = jnp.where(row < lane, mixed, jnp.where(row > lane, turned, diag))
    cells = FIELDS * SHARE

    def dot(a, b, da, db):
        return lax.dot_general(
            a,
            b,
            (((da,), (db,)), ((), ())),
            precision=EXACT,
            preferred_element_type=jnp.float32,
        )

    def put(x, h):
        for f in range(FIELDS):
            basis_ref[pl.ds(2 * f + h, SHARE, stride=2 * FIELDS), :] = x[
                SHARE * f : SHARE * f + SHARE
            ]

    groups = range(HALF // 8)
    uppers, lowers = factor([first[8 * t : 8 * t + 8] for t in groups])
    low_a = jnp.concatenate(lowers, axis=0)
    upper_ref[:HALF, :HALF] = jnp.concatenate(uppers, axis=0)
    side = dot(low_a, cross, 1, 1)
    last = last - dot(side, side, 0, 0)
    upper_ref[:HALF, HALF:] = side
    upper_ref[HALF:, :HALF] = jnp.zeros((HALF, HALF), jnp.float32)
    basis_a = dot(panel_ref[:, :, :HALF].reshape(cells, HALF), low_a, 1, 1)
    rest = panel_ref[:, :, HALF:].reshape(cells, HALF) - dot(basis_a, side, 1, 0)
    put(basis_a, 0)
    uppers, lowers = factor([last[8 * t : 8 * t + 8] for t in groups])
    low_b = jnp.concatenate(lowers, axis=0)
    upper_ref[HALF:, HALF:] = jnp.concatenate(uppers, axis=0)
    put(dot(rest, low_b, 1, 1), 1)


def basis_call(gram, panel):
    vmem = pl.BlockSpec(memory_space=pltpu.VMEM)
    basis, upper = pl.pallas_call(
        basis_kernel,
        in_specs=[vmem, vmem],
        out_specs=[vmem, vmem],
        out_shape=[
            jax.ShapeDtypeStruct((SHARE * FIELDS * 2, HALF), jnp.float32),
            jax.ShapeDtypeStruct((RANK, RANK), jnp.float32),
        ],
        compiler_params=pltpu.CompilerParams(vmem_limit_bytes=32 * 2**20),
    )(gram, panel)
    return basis.reshape(SHARE, FIELDS, 1, RANK), upper


def swap(x, axis, mask):
    return lax.ppermute(x, axis, [(i, i ^ mask) for i in range(lax.axis_size(axis))])


def permute(x, target):
    pairs = []
    for source in range(2 * 4 * NZ):
        tm, space = divmod(source, NZ)
        y, core, gx, gz = target(tm >> 1, tm & 1, space >> 3, space & 7)
        pairs.append((source, (2 * y + core) * NZ + 8 * gx + gz))
    return lax.ppermute(x, ("tm", "space"), pairs)


def step_swap(x, which):
    return permute(
        x, lambda y, c, gx, gz: (y ^ step_masks(c ^ (y & 1))[which], c ^ 1, gx, gz)
    )


def halo_swap(x, which):
    def target(y, c, gx, gz):
        plane = 8 * gx + gz
        if c == which:
            goal = plane ^ 1
        else:
            goal = plane + 1 if plane & 1 else plane - 1
        return (y, c, goal >> 3, goal & 7) if 0 <= goal < NZ else (y ^ 1, c, gx, gz)

    return permute(x, target)


def sum_along_y(mine):
    mine = mine[:2] + step_swap(mine[2:], 0)
    return mine[0] + step_swap(mine[1], 1)


def parity(y, x, z):
    return (y ^ x ^ z ^ (z >> 1)) & 1


def gram_swap(x, masks):
    def target(y, c, gx, gz):
        dy, dx, dz = masks[c ^ parity(y, gx, gz)]
        return y ^ dy, c ^ parity(dy, dx, dz), gx ^ dx, gz ^ dz

    return permute(x, target)


def sum_over_all(gram):
    tm, space = lax.axis_index("tm"), lax.axis_index("space")
    side = (tm & 1) ^ parity(tm >> 1, space >> 3, space & 7)
    n = gram.shape[0] // 2
    mine = lax.dynamic_slice_in_dim(gram, side * n, n, 0)
    other = lax.dynamic_slice_in_dim(gram, (1 - side) * n, n, 0)
    mine = mine + swap(other, "tm", 1)
    for step in GRAM_STEPS:
        mine = mine + functools.reduce(jnp.add, [gram_swap(mine, masks) for masks in step])
    other = swap(mine, "tm", 1)
    return jnp.where(
        side == 0, jnp.concatenate([mine, other], 0), jnp.concatenate([other, mine], 0)
    )


PARTS = ((0, 6, 6), (6, 6, 0))
def single(a, b):
    return ((a, b),)


def four(a, b):
    both = [tuple(i ^ j for i, j in zip(*pair)) for pair in (a, b)]
    return (a[0], b[0]), (a[1], b[1]), (both[0], both[1])


Y1, Y3 = (1, 0, 0), (3, 0, 0)
X1, X3 = (0, 1, 0), (0, 3, 0)
Z1, Z2, Z6 = (0, 0, 1), (0, 0, 2), (0, 0, 6)
GRAM_STEPS = (
    single(Y3, Z6),
    single(X3, Y3),
    single(Z6, X3),
    four((Y1, X1), (Z1, Z2)),
    four((Z1, Z2), (Y1, X1)),
)


def shards(snapshots, sketch, volume, grad_weight, dilation):
    snaps = jnp.transpose(snapshots[:, :, 0, :], (1, 0, 2))
    parts = []
    for first, count, later in PARTS:
        send, keep, *snaps = sketch_call(
            snaps, sketch, dilation, grad_weight, first, count, later
        )
        snaps = snaps[0] if snaps else None
        image = sum_along_y(keep + swap(send, "tm", 1))
        parts += [image, halo_swap(image, 0), halo_swap(image, 1)]
    panel, gram = panel_call(volume, [p.shape[0] for p in parts[::3]], parts)
    gram = sum_over_all(gram)
    basis, upper = basis_call(gram, panel)
    return basis, upper


def solution(mesh):
    return jax.shard_map(
        shards,
        mesh=mesh,
        in_specs=(P("tm", None, "space", None), P("tm", None), P("space", None), P(), P()),
        out_specs=(P("tm", None, "space", None), P()),
        check_vma=False,
    )
```

```python
import functools

import jax
import jax.numpy as jnp
from jax import lax
from jax.experimental import pallas as pl
from jax.experimental.pallas import tpu as pltpu
from jax.sharding import PartitionSpec as P

WX = 16
WY = 16
PLANE = WX * WY
RANK = 256
FIELDS = 12
SHARE = 32
SNAP_DEV = 1024
NZ = 32
ROWS = 98304
HALF = 128
GROUP = 4
DILATIONS = 4
EXACT = lax.Precision.HIGHEST


def hat(offset):
    return jnp.maximum(0.5 - 0.25 * jnp.abs(offset), 0.0)


def hat_slope(source, target, shift):
    ahead = jnp.where(target + shift < 16.0, hat(source - target - shift), 0.0)
    behind = jnp.where(target - shift >= 0.0, hat(source - target + shift), 0.0)
    return 0.5 * (ahead - behind)


def filter_tables(table, blocks):
    lane = lax.broadcasted_iota(jnp.int32, (WX, PLANE), 1)
    px = (lane & 15).astype(jnp.float32)
    py = (lane >> 4).astype(jnp.float32)
    qx = lax.broadcasted_iota(jnp.int32, (WX, PLANE), 0).astype(jnp.float32)
    along_x = hat(px - qx)
    slopes = [hat_slope(px, qx, float(d + 1)) for d in range(DILATIONS)]
    for r, block in enumerate(blocks):
        for h in range(2):
            qy = jnp.full((WX, PLANE), (2 * block + h).astype(jnp.float32))
            rows = pl.ds(32 * r + 16 * h, 16)
            along_y = hat(py - qy)
            table[0, rows, :] = (along_y * along_x).astype(jnp.bfloat16)
            for d in range(DILATIONS):
                mixed = along_y * slopes[d] + hat_slope(py, qy, float(d + 1)) * along_x
                table[d + 1, rows, :] = mixed.astype(jnp.bfloat16)


def step_masks(side):
    return 1 + 2 * side, 3 - 2 * side


def step_blocks(y, core):
    near, far = step_masks(core ^ (y & 1))
    return [2 * (y ^ m) + (core ^ (m & 1)) for m in (0, far, near, near ^ far)]


def split(x):
    high = x.astype(jnp.bfloat16)
    return high, (x - high.astype(jnp.float32)).astype(jnp.bfloat16)


def sketch_kernel(first, count, later, snap_ref, sketch_hbm, shift_hbm, weight_hbm, *refs):
    held_refs = refs[2 : 2 + (later > 0)]
    send_ref, keep_ref = refs[:2]
    snap, sketch, turned, table, shift, weight, snap_sem, sem = refs[2 + (later > 0) :]
    heads = [
        pltpu.make_async_copy(sketch_hbm, sketch, sem.at[0]),
        pltpu.make_async_copy(shift_hbm, shift, sem.at[1]),
        pltpu.make_async_copy(weight_hbm, weight, sem.at[2]),
    ]
    copies = []
    if later:
        places = [snap.at[f] for f in range(count)] + [held_refs[0].at[f] for f in range(later)]
        copies = [
            pltpu.make_async_copy(snap_ref.at[f], place, snap_sem.at[f])
            for f, place in enumerate(places)
        ]
    else:
        snap = snap_ref
    for copy in heads + copies:
        copy.start()
    me = lax.axis_index("tm")
    y, core = me // 2, me % 2
    filter_tables(table, step_blocks(y, 1 - core) + step_blocks(y, core))
    for copy in heads:
        copy.wait()
    turned[...] = sketch[...].T
    dot = functools.partial(
        lax.dot_general,
        dimension_numbers=(((1,), (1,)), ((), ())),
        preferred_element_type=jnp.float32,
    )

    def filtered(f, raw):
        high, low = split(raw)
        blur, slope = table[0], table[shift[first + f]]
        image = (dot(blur, high) + dot(blur, low)) + weight[first + f] * (
            dot(slope, high) + dot(slope, low)
        )
        send_ref[:, f] = image[:HALF].reshape(4, SHARE, RANK)
        keep_ref[:, f] = image[HALF:].reshape(4, SHARE, RANK)

    held = None
    for g in range(0, count + GROUP, GROUP):
        if g < count:
            for copy in copies[g : g + GROUP]:
                copy.wait()
            raws = [
                jnp.dot(turned[...], snap[f], preferred_element_type=jnp.float32)
                for f in range(g, g + GROUP)
            ]
        if held is not None:
            for k in range(GROUP):
                filtered(g - GROUP + k, held[k])
        held = raws
    for copy in copies[count:]:
        copy.wait()


def sketch_call(snaps, sketch, dilation, weight, first, count, later):
    out = jax.ShapeDtypeStruct((4, count, SHARE, RANK), jnp.float32)
    hbm = pl.BlockSpec(memory_space=pltpu.HBM)
    vmem = pl.BlockSpec(memory_space=pltpu.VMEM)
    rest = [jax.ShapeDtypeStruct((later, SNAP_DEV, PLANE), jnp.bfloat16)] if later else []
    return pl.pallas_call(
        functools.partial(sketch_kernel, first, count, later),
        in_specs=[hbm if later else vmem] + [hbm] * 3,
        out_specs=[vmem] * (2 + len(rest)),
        out_shape=[out] * 2 + rest,
        scratch_shapes=[
            pltpu.VMEM((count if later else 1, SNAP_DEV, PLANE), jnp.bfloat16),
            pltpu.VMEM((SNAP_DEV, RANK), jnp.bfloat16),
            pltpu.VMEM((RANK, SNAP_DEV), jnp.bfloat16),
            pltpu.VMEM((DILATIONS + 1, PLANE, PLANE), jnp.bfloat16),
            pltpu.SMEM((FIELDS,), jnp.int32),
            pltpu.SMEM((FIELDS,), jnp.float32),
            pltpu.SemaphoreType.DMA((count + later,)),
            pltpu.SemaphoreType.DMA((3,)),
        ],
        compiler_params=pltpu.CompilerParams(vmem_limit_bytes=46 * 2**20),
        cost_estimate=pl.CostEstimate(
            flops=count * 2**28, bytes_accessed=count * 2**20, transcendentals=0
        ),
    )(snaps, sketch, dilation, weight)


def panel_kernel(counts, volume_ref, *refs):
    parts, (panel_ref, gram_ref) = refs[:-2], refs[-2:]
    me, plane = lax.axis_index("tm"), lax.axis_index("space")
    inner = (plane > 0) & (plane < NZ - 1)
    use_first, use_second = inner | (me % 2 == 0), inner | (me % 2 == 1)
    row = lax.broadcasted_iota(jnp.int32, (SHARE, PLANE), 0)
    lane = lax.broadcasted_iota(jnp.int32, (SHARE, PLANE), 1)
    volume = jnp.broadcast_to(volume_ref[...], (SHARE, PLANE))
    mine = jnp.sum(jnp.where(lane == row + me * SHARE, volume, 0.0), axis=1, keepdims=True)
    root = jnp.broadcast_to(jnp.sqrt(mine), (SHARE, RANK))
    scaled = []
    at = 0
    for n, count in enumerate(counts):
        here, first, second = parts[3 * n : 3 * n + 3]
        for f in range(count):
            panel = 0.5 * here[f]
            panel = panel + jnp.where(use_first, 0.25 * first[f], 0.0)
            panel = panel + jnp.where(use_second, 0.25 * second[f], 0.0)
            panel_ref[at] = panel
            scaled.append(panel * root)
            at += 1
    rows = jnp.concatenate(scaled, axis=0)
    gram = lax.dot_general(
        rows,
        rows,
        (((0,), (0,)), ((), ())),
        precision=EXACT,
        preferred_element_type=jnp.float32,
    )
    gram = gram * (1.0 / ROWS)
    gram_ref[:HALF] = gram[HALF:, :HALF]
    row = lax.broadcasted_iota(jnp.int32, (HALF, HALF), 0)
    lane = lax.broadcasted_iota(jnp.int32, (HALF, HALF), 1)
    last = gram[HALF:, HALF:]
    gram_ref[HALF : 2 * HALF] = jnp.where(row >= lane, gram[:HALF, :HALF], last)
    diag = jnp.sum(jnp.where(row == lane, last, 0.0), axis=0, keepdims=True)
    gram_ref[2 * HALF :] = jnp.broadcast_to(diag, (16, HALF))


def panel_call(volume, counts, parts):
    vmem = pl.BlockSpec(memory_space=pltpu.VMEM)
    return pl.pallas_call(
        functools.partial(panel_kernel, counts),
        in_specs=[vmem] * (1 + len(parts)),
        out_specs=[vmem, vmem],
        out_shape=[
            jax.ShapeDtypeStruct((FIELDS, SHARE, RANK), jnp.float32),
            jax.ShapeDtypeStruct((272, HALF), jnp.float32),
        ],
        compiler_params=pltpu.CompilerParams(vmem_limit_bytes=16 * 2**20),
    )(volume, *parts)


def total(terms):
    terms = list(terms)
    while len(terms) > 1:
        terms = [a + b for a, b in zip(terms[::2], terms[1::2])] + (
            terms[-1:] if len(terms) % 2 else []
        )
    return terms[0]


def factor(rows):
    shape = (8, HALF)
    sub = lax.broadcasted_iota(jnp.int32, shape, 0)
    lane = lax.broadcasted_iota(jnp.int32, shape, 1)
    rows = list(rows)
    count = len(rows)
    uppers, lowers = [], []
    at = [sub == j for j in range(8)]

    def column(x, j):
        return jnp.broadcast_to(x[:, j : j + 1], shape)

    def row_of(x, i):
        return jnp.broadcast_to(x[i : i + 1, :], shape)

    cols = [column(rows[0], m) for m in range(8)]
    for s in range(count):
        here = rows[s]
        there = jnp.where(lane == sub + 8 * s, 1.0, 0.0)
        inside = (lane >= 8 * s) & (lane < 8 * s + 8)
        last = s + 1 == count
        ahead = [] if last else [column(here, 8 * s + 8 + m) for m in range(8)]
        upper = lower = jnp.zeros(shape, jnp.float32)
        for j in range(0, 8, 2):
            p, q = cols[j], cols[j + 1]
            a, b, c = row_of(p, j), row_of(q, j), row_of(q, j + 1)
            det = a * c - b * b
            inv_det = 1.0 / det
            inv_a = 1.0 / a
            root_a, root_c = lax.rsqrt(a), lax.rsqrt(det * inv_a)
            slope = b * inv_a
            into_a, into_b, into_c = a * inv_det, b * inv_det, c * inv_det

            def eliminate(x):
                x0, x1 = row_of(x, j), row_of(x, j + 1)
                y0 = into_c * x0 - into_b * x1
                y1 = into_a * x1 - into_b * x0
                return jnp.where(at[j], y0, jnp.where(at[j + 1], y1, x - p * y0 - q * y1))

            def factored(x, kept):
                x0, x1 = row_of(x, j), row_of(x, j + 1)
                second = (x1 - slope * x0) * root_c
                return jnp.where(at[j], x0 * root_a, jnp.where(at[j + 1], second, kept))

            upper, lower = factored(here, upper), factored(there, lower)
            here, there = eliminate(here), eliminate(there)
            for m in range(j + 2, 8):
                cols[m] = eliminate(cols[m])
            ahead = [eliminate(x) for x in ahead]
        uppers.append(jnp.where(lane >= sub + 8 * s, upper, 0.0))
        lowers.append(jnp.where(inside, lower, jnp.where(lane < 8 * s, upper, 0.0)))
        if last:
            break
        weights = [column(rows[s + 1], 8 * s + m) for m in range(8)]
        cols = [
            column(rows[s + 1], 8 * s + 8 + m)
            - total(weights[k] * row_of(ahead[m], k) for k in range(8))
            for m in range(8)
        ]
        solved = jnp.where(inside, there, here)
        solved_rows = [row_of(solved, m) for m in range(8)]
        for t in range(s + 1, count):
            if t > s + 1:
                weights = [column(rows[t], 8 * s + m) for m in range(8)]
            rows[t] = jnp.where(inside, 0.0, rows[t]) - total(
                weights[m] * solved_rows[m] for m in range(8)
            )
    return uppers, lowers


def basis_kernel(gram_ref, panel_ref, basis_ref, upper_ref):
    row = lax.broadcasted_iota(jnp.int32, (HALF, HALF), 0)
    lane = lax.broadcasted_iota(jnp.int32, (HALF, HALF), 1)
    cross = gram_ref[:HALF]
    mixed = gram_ref[HALF : 2 * HALF]
    turned = mixed.T
    first = jnp.where(row >= lane, mixed, turned)
    diag = jnp.broadcast_to(gram_ref[2 * HALF : 2 * HALF + 1, :], (HALF, HALF))
    last = jnp.where(row < lane, mixed, jnp.where(row > lane, turned, diag))
    cells = FIELDS * SHARE

    def dot(a, b, da, db):
        return lax.dot_general(
            a,
            b,
            (((da,), (db,)), ((), ())),
            precision=EXACT,
            preferred_element_type=jnp.float32,
        )

    def put(x, h):
        for f in range(FIELDS):
            basis_ref[pl.ds(2 * f + h, SHARE, stride=2 * FIELDS), :] = x[
                SHARE * f : SHARE * f + SHARE
            ]

    groups = range(HALF // 8)
    uppers, lowers = factor([first[8 * t : 8 * t + 8] for t in groups])
    low_a = jnp.concatenate(lowers, axis=0)
    upper_ref[:HALF, :HALF] = jnp.concatenate(uppers, axis=0)
    side = dot(low_a, cross, 1, 1)
    last = last - dot(side, side, 0, 0)
    upper_ref[:HALF, HALF:] = side
    upper_ref[HALF:, :HALF] = jnp.zeros((HALF, HALF), jnp.float32)
    basis_a = dot(panel_ref[:, :, :HALF].reshape(cells, HALF), low_a, 1, 1)
    rest = panel_ref[:, :, HALF:].reshape(cells, HALF) - dot(basis_a, side, 1, 0)
    put(basis_a, 0)
    uppers, lowers = factor([last[8 * t : 8 * t + 8] for t in groups])
    low_b = jnp.concatenate(lowers, axis=0)
    upper_ref[HALF:, HALF:] = jnp.concatenate(uppers, axis=0)
    put(dot(rest, low_b, 1, 1), 1)


def basis_call(gram, panel):
    vmem = pl.BlockSpec(memory_space=pltpu.VMEM)
    basis, upper = pl.pallas_call(
        basis_kernel,
        in_specs=[vmem, vmem],
        out_specs=[vmem, vmem],
        out_shape=[
            jax.ShapeDtypeStruct((SHARE * FIELDS * 2, HALF), jnp.float32),
            jax.ShapeDtypeStruct((RANK, RANK), jnp.float32),
        ],
        compiler_params=pltpu.CompilerParams(vmem_limit_bytes=32 * 2**20),
    )(gram, panel)
    return basis.reshape(SHARE, FIELDS, 1, RANK), upper


def swap(x, axis, mask):
    return lax.ppermute(x, axis, [(i, i ^ mask) for i in range(lax.axis_size(axis))])


def permute(x, target):
    pairs = []
    for source in range(2 * 4 * NZ):
        tm, space = divmod(source, NZ)
        y, core, gx, gz = target(tm >> 1, tm & 1, space >> 3, space & 7)
        pairs.append((source, (2 * y + core) * NZ + 8 * gx + gz))
    return lax.ppermute(x, ("tm", "space"), pairs)


def step_swap(x, which):
    return permute(
        x, lambda y, c, gx, gz: (y ^ step_masks(c ^ (y & 1))[which], c ^ 1, gx, gz)
    )


def halo_swap(x, which):
    def target(y, c, gx, gz):
        plane = 8 * gx + gz
        if c == which:
            goal = plane ^ 1
        else:
            goal = plane + 1 if plane & 1 else plane - 1
        return (y, c, goal >> 3, goal & 7) if 0 <= goal < NZ else (y ^ 1, c, gx, gz)

    return permute(x, target)


def sum_along_y(mine):
    mine = mine[:2] + step_swap(mine[2:], 0)
    return mine[0] + step_swap(mine[1], 1)


def parity(y, x, z):
    return (y ^ x ^ z ^ (z >> 1)) & 1


def gram_swap(x, masks):
    def target(y, c, gx, gz):
        dy, dx, dz = masks[c ^ parity(y, gx, gz)]
        return y ^ dy, c ^ parity(dy, dx, dz), gx ^ dx, gz ^ dz

    return permute(x, target)


def sum_over_all(gram):
    tm, space = lax.axis_index("tm"), lax.axis_index("space")
    side = (tm & 1) ^ parity(tm >> 1, space >> 3, space & 7)
    n = gram.shape[0] // 2
    mine = lax.dynamic_slice_in_dim(gram, side * n, n, 0)
    other = lax.dynamic_slice_in_dim(gram, (1 - side) * n, n, 0)
    mine = mine + swap(other, "tm", 1)
    for step in GRAM_STEPS:
        mine = mine + functools.reduce(jnp.add, [gram_swap(mine, masks) for masks in step])
    other = swap(mine, "tm", 1)
    return jnp.where(
        side == 0, jnp.concatenate([mine, other], 0), jnp.concatenate([other, mine], 0)
    )


PARTS = ((0, 8, 4), (8, 4, 0))
def single(a, b):
    return ((a, b),)


def four(a, b):
    both = [tuple(i ^ j for i, j in zip(*pair)) for pair in (a, b)]
    return (a[0], b[0]), (a[1], b[1]), (both[0], both[1])


Y1, Y3 = (1, 0, 0), (3, 0, 0)
X1, X3 = (0, 1, 0), (0, 3, 0)
Z1, Z2, Z6 = (0, 0, 1), (0, 0, 2), (0, 0, 6)
GRAM_STEPS = (
    single(Y3, Z6),
    single(X3, Y3),
    single(Z6, X3),
    four((Y1, X1), (Z1, Z2)),
    four((Z1, Z2), (Y1, X1)),
)


def shards(snapshots, sketch, volume, grad_weight, dilation):
    snaps = jnp.transpose(snapshots[:, :, 0, :], (1, 0, 2))
    parts = []
    for first, count, later in PARTS:
        send, keep, *snaps = sketch_call(
            snaps, sketch, dilation, grad_weight, first, count, later
        )
        snaps = snaps[0] if snaps else None
        image = sum_along_y(keep + swap(send, "tm", 1))
        parts += [image, halo_swap(image, 0), halo_swap(image, 1)]
    panel, gram = panel_call(volume, [p.shape[0] for p in parts[::3]], parts)
    gram = sum_over_all(gram)
    basis, upper = basis_call(gram, panel)
    return basis, upper


def solution(mesh):
    return jax.shard_map(
        shards,
        mesh=mesh,
        in_specs=(P("tm", None, "space", None), P("tm", None), P("space", None), P(), P()),
        out_specs=(P("tm", None, "space", None), P()),
        check_vma=False,
    )
```
